256 devices in a mesh: queue: 16 (over x_lo, z), seq: 16 (over y, x_hi, core).
Axes of the slice: x: 4 (x_hi: 2, x_lo: 2; x = x_hi * 2 + x_lo), y: 4, z: 8, core: 2. Of those that a mesh axis runs over, the one named last changes fastest.
Arguments:
- latents: float32 [32, 1024, 16], P('queue', 'seq'), may hold values from -6 to 6
- levels: int32 [32], P('queue'), may hold values from 0 to 31, as said below
- advance: int32 [16], P('queue'), may hold values from 1 to 2, as said below
- fresh_noise: float32 [1024, 16], P('seq'), may hold values from -6 to 6
- level_mod: float32 [32, 8, 1152], P(None, None, 'seq'), may hold values from -4 to 4
- embed_w: float32 [16, 1152], replicated, may hold values from -1.5 to 1.5
- spatial_qkv: bfloat16 [1152, 3, 1152], replicated
- spatial_out: bfloat16 [1152, 1152], P(None, 'seq'), may hold values from -0.1875 to 0.1875
- temporal_qkv: bfloat16 [1152, 3, 1152], P(None, None, 'seq')
- temporal_out: bfloat16 [1152, 1152], P(None, 'seq'), may hold values from -0.1875 to 0.1875
- final_w: bfloat16 [1152, 16], replicated, may hold values from -0.1875 to 0.1875
Outputs:
- velocity: float32 [32, 1024, 16], P('queue', 'seq')
- queue_next: float32 [32, 1024, 16], P('queue', 'seq')
The draws below stay inside these ranges and needn't reach their ends.
Inputs may be any that keep to these rules, and one draw needn't show every extreme that they name: `levels`: the level of slot f lies within 2 of f; the first slot has level 0 and the last level 31. `advance`: some window other than the last takes all 2 frames; the last window's entry is not used.
All inputs are finite; a program needn't handle non-finite values.
Results may differ from the reference program's by a relative error of at most 0.02.
Values may be sent and summed in bfloat16 or wider, within the bound.
No kernel may reach another device: no remote copies, remote signals or barrier semaphores. Data moves between devices by JAX's collectives and lax.ppermute only.
A program may use at most 128 MiB of HBM per device.

```python
import math
import jax
import jax.numpy as jnp
from jax import lax

D = 1152
HEADS = 16
HD = 72
PC = 16
FW = 2
S = 1024
FRAMES = 32
N_QUEUE = 16


def draw_levels(key, part):
    key = jax.random.fold_in(key, 1)
    slots = jnp.arange(FRAMES, dtype=jnp.int32)
    jitter = jax.random.randint(key, (FRAMES,), -2, 3, dtype=jnp.int32)
    level = jnp.clip(slots + jitter, 0, FRAMES - 1)
    level = jnp.where(slots == 0, 0, level)
    return jnp.where(slots == FRAMES - 1, FRAMES - 1, level).astype(jnp.int32)


def draw_advance(key, part):
    key = jax.random.fold_in(key, 2)
    first_key, second_key = jax.random.split(key)
    counts = jax.random.randint(first_key, (N_QUEUE,), 1, FW + 1, dtype=jnp.int32)
    chosen = jax.random.randint(second_key, (), 0, max(N_QUEUE - 1, 1), dtype=jnp.int32)
    window_ids = jnp.arange(N_QUEUE, dtype=jnp.int32)
    return jnp.where(window_ids == chosen, FW, counts).astype(jnp.int32)


def draw_spatial_qkv(key, part):
    key = jax.random.fold_in(key, 3)
    weight = jax.random.normal(key, (D, 3, D), jnp.float32) * (1.7 / math.sqrt(D))
    return weight.astype(jnp.bfloat16)


def draw_temporal_qkv(key, part):
    key = jax.random.fold_in(key, 4)
    weight = jax.random.normal(key, (D, 3, D), jnp.float32) * (1.7 / math.sqrt(D))
    return weight.astype(jnp.bfloat16)


def block_scale(key, shape, cuts, low, largest):
    def one(axis_at, parts):
        draws = jax.random.uniform(jax.random.fold_in(jax.random.fold_in(key, 6), axis_at), (parts,), jnp.float32, low / len(cuts), largest / len(cuts))
        return jnp.repeat(jnp.exp(draws), shape[axis_at] // parts).reshape((-1,) + (1,) * (len(shape) - axis_at - 1))

    factor_of = one(*cuts[0])
    for cut in cuts[1:]:
        factor_of = factor_of * one(*cut)
    return factor_of


def centred(own_key, dims, scale, bound, shards=(), held_as=jnp.bfloat16):
    values = scale * jax.random.normal(own_key, dims, jnp.float32)
    if shards:
        values = values * block_scale(own_key, dims, shards, -0.22, 0.18)
    return jnp.clip(values, -bound, bound).astype(held_as)


def setup_inputs(seed: int = 0) -> dict:
    seeds = jax.random.split(jax.random.key(seed), 12)
    return {
        "latents": centred(seeds[0], (FRAMES, S, PC), 1.0, 6.0, ((0, 16), (1, 16)), jnp.float32),
        "levels": draw_levels(jax.random.fold_in(seeds[11], 71), 0),
        "advance": draw_advance(jax.random.fold_in(seeds[11], 71), 0),
        "fresh_noise": centred(seeds[3], (S, PC), 1.0, 6.0, ((0, 16),), jnp.float32),
        "level_mod": centred(seeds[4], (FRAMES, 8, D), 0.7, 4.0, ((2, 16),), jnp.float32),
        "embed_w": centred(seeds[5], (PC, D), PC ** -0.5, 1.5, (), jnp.float32),
        "spatial_qkv": draw_spatial_qkv(jax.random.fold_in(seeds[11], 71), 0),
        "spatial_out": centred(seeds[7], (D, D), D ** -0.5, 0.1875, ((1, 16),)),
        "temporal_qkv": draw_temporal_qkv(jax.random.fold_in(seeds[11], 71), 0),
        "temporal_out": centred(seeds[9], (D, D), D ** -0.5, 0.1875, ((1, 16),)),
        "final_w": centred(seeds[10], (D, PC), D ** -0.5, 0.1875),
    }


def layer_norm(hidden):
    mean_value = lax.optimization_barrier(jnp.mean(hidden, axis=-1, keepdims=True))
    centered = hidden - mean_value
    variance = lax.optimization_barrier(jnp.mean(centered * centered, axis=-1, keepdims=True))
    return centered * lax.rsqrt(variance + 1e-06)

def modulate(hidden, modulation, index):
    return layer_norm(hidden) * (1.0 + modulation[:, None, index + 1]) + modulation[:, None, index]

def project(inputs, weight):
    flat_in = inputs.reshape(-1, inputs.shape[-1])
    return jnp.dot(flat_in, weight.reshape(weight.shape[0], -1), preferred_element_type=jnp.float32)

def spatial_frame(frame_block):
    scale_value = 1.0 / math.sqrt(HD)
    query_part = frame_block[:, 0].astype(jnp.float32)
    key_part = frame_block[:, 1].astype(jnp.float32)
    value_part = frame_block[:, 2].astype(jnp.float32)
    scores = jnp.einsum('qhe,khe->hqk', query_part, key_part) * scale_value
    attn_probs = jax.nn.softmax(scores, axis=-1).astype(jnp.bfloat16)
    return jnp.einsum('hqk,khe->qhe', attn_probs.astype(jnp.float32), value_part).astype(jnp.bfloat16)

def reference(latents, levels, advance, fresh_noise, level_mod, embed_w, spatial_qkv, spatial_out, temporal_qkv, temporal_out, final_w):
    modulation = level_mod[levels]
    embedded = jnp.einsum('fsc,cd->fsd', latents, embed_w, precision=lax.Precision.HIGHEST)
    spatial_in = modulate(embedded, modulation, 0).astype(jnp.bfloat16)
    spatial_proj = project(spatial_in, spatial_qkv).astype(jnp.bfloat16).reshape(FRAMES, S, 3, HEADS, HD)
    spatial_mix = lax.map(spatial_frame, spatial_proj).reshape(FRAMES, S, D)
    hidden_one = embedded + modulation[:, None, 2] * project(spatial_mix, spatial_out).reshape(FRAMES, S, D)
    temporal_in = modulate(hidden_one, modulation, 3).astype(jnp.bfloat16)
    temporal_proj = project(temporal_in, temporal_qkv).astype(jnp.bfloat16).reshape(N_QUEUE, FW, S, 3, HEADS, HD)
    ahead = jnp.concatenate([temporal_proj[1:, :, :, 1:], jnp.zeros_like(temporal_proj[:1, :, :, 1:])], axis=0)
    window_ids = jnp.arange(N_QUEUE, dtype=jnp.int32)
    limits = jnp.where(window_ids == N_QUEUE - 1, 0, advance).astype(jnp.int32)
    scale_value = 1.0 / math.sqrt(HD)

    def temporal_window(packed):
        own, following, limit = packed
        query_part = own[:, :, 0].astype(jnp.float32)
        key_part = jnp.concatenate([own[:, :, 1], following[:, :, 0]], axis=0).astype(jnp.float32)
        value_part = jnp.concatenate([own[:, :, 2], following[:, :, 1]], axis=0).astype(jnp.float32)
        scores = jnp.einsum('ishe,jshe->shij', query_part, key_part) * scale_value
        column = jnp.arange(2 * FW, dtype=jnp.int32)
        keep = (column < FW) | (column - FW < limit)
        scores = jnp.where(keep, scores, -jnp.inf)
        attn_probs = jax.nn.softmax(scores, axis=-1).astype(jnp.bfloat16)
        return jnp.einsum('shij,jshe->ishe', attn_probs.astype(jnp.float32), value_part).astype(jnp.bfloat16)
    temporal_mix = lax.map(temporal_window, (temporal_proj, ahead, limits)).reshape(FRAMES, S, D)
    hidden_two = hidden_one + modulation[:, None, 5] * project(temporal_mix, temporal_out).reshape(FRAMES, S, D)
    final_in = modulate(hidden_two, modulation, 6).astype(jnp.bfloat16)
    velocity = project(final_in, final_w).reshape(FRAMES, S, PC)
    updated = latents - velocity / FRAMES
    queue_next = jnp.concatenate([updated[1:], fresh_noise[None]], axis=0)
    return (velocity, queue_next)
```

```python
import math

import jax
import jax.numpy as jnp
from jax import lax
from jax.experimental import pallas as pl
from jax.experimental.pallas import tpu as pltpu
from jax.sharding import PartitionSpec as P

HEADS = 16
HD = 72
D = HEADS * HD
C = 16
CP = 32
BF = jnp.bfloat16
F32 = jnp.float32
VMEM = pl.BlockSpec(memory_space=pltpu.VMEM)
SMEM = pl.BlockSpec(memory_space=pltpu.SMEM)


def split(value):
    high = value.astype(BF)
    return high, (value - high.astype(F32)).astype(BF)


def dot_tn(a, b):
    return lax.dot_general(a, b, (((0,), (0,)), ((), ())), preferred_element_type=F32)


def dot_nt(a, b):
    return lax.dot_general(a, b, (((1,), (1,)), ((), ())), preferred_element_type=F32)


def dot_nn(a, b):
    return jnp.dot(a, b, preferred_element_type=F32)


def product_tn(a, b):
    a_high, a_low = split(a)
    b_high, b_low = split(b)
    return dot_tn(
        jnp.concatenate([a_high, a_low, a_high], axis=0),
        jnp.concatenate([b_high, b_high, b_low], axis=0),
    )


def both_frames(latents_ref):
    return jnp.concatenate([latents_ref[0], latents_ref[1]], axis=1)


def normalize(hidden):
    width = hidden.shape[0]
    mean_value = jnp.sum(hidden, axis=0, keepdims=True) * (1.0 / width)
    centered = hidden - mean_value
    variance = jnp.sum(centered * centered, axis=0, keepdims=True) * (1.0 / width)
    return centered * lax.rsqrt(variance + 1e-06)


def modulation_columns(mod, rows):
    tokens = 128
    high, low = split(mod)
    row_at = lax.broadcasted_iota(jnp.int32, (16, tokens * len(rows)), 0)
    lane_at = lax.broadcasted_iota(jnp.int32, (16, tokens * len(rows)), 1)
    wanted = jnp.zeros_like(row_at)
    for place, row in enumerate(rows):
        wanted = jnp.where(lane_at // tokens == place, row, wanted)
    wanted = wanted + 8 * ((lane_at % tokens) // 64)
    chosen = (row_at == wanted).astype(F32).astype(BF)
    columns = dot_tn(
        jnp.concatenate([high, low], axis=0), jnp.concatenate([chosen, chosen], axis=0)
    )
    return [columns[:, tokens * i : tokens * (i + 1)] for i in range(len(rows))]


def pack_kernel(levels_ref, latents_ref, embed_ref, table_ref, out_ref):
    channels = both_frames(latents_ref)
    embed = embed_ref[...]
    centered = embed - jnp.sum(embed, axis=1, keepdims=True) * (1.0 / D)
    spread = product_tn(centered, channels)
    variance = jnp.sum(spread * spread, axis=0, keepdims=True) * (1.0 / D)
    scaled = channels * lax.rsqrt(variance + 1e-06)
    peers = out_ref.shape[0]
    for peer in range(peers):
        out_ref[peer, 0:16, :] = scaled
        for frame in range(2):
            rows = table_ref[levels_ref[frame]]
            out_ref[peer, 16 + 8 * frame : 24 + 8 * frame, 0:HD] = rows


def spatial_kernel(own_ref, all_ref, embed_ref, weight_ref, mix_ref, mod_ref, tokens_ref, query_ref, part_ref):
    peers = all_ref.shape[0]
    for peer in range(peers):
        mod_ref[:, HD * peer : HD * (peer + 1)] = all_ref[peer, 16:32, 0:HD]
        for frame in range(2):
            tokens_ref[frame, :, 64 * peer : 64 * (peer + 1)] = all_ref[
                peer, 0:16, 64 * frame : 64 * (frame + 1)
            ]
    mod = mod_ref[...]
    embed = embed_ref[...]
    centered = embed - jnp.sum(embed, axis=1, keepdims=True) * (1.0 / D)
    row16 = lax.broadcasted_iota(jnp.int32, (16, D), 0)
    rows = []
    for frame in range(2):
        rows.append(centered * (1.0 + mod[8 * frame + 1 : 8 * frame + 2]))
        rows.append(jnp.where(row16 == 0, mod[8 * frame : 8 * frame + 1], 0.0))
    high, low = split(jnp.concatenate(rows, axis=0))
    stacked = jnp.concatenate([high, low], axis=0)

    def coefficients(index):
        both = dot_nn(stacked, weight_ref[index])
        return both[0:64] + both[64:128]

    query_all = coefficients(0)
    key_all = coefficients(1)
    value_all = coefficients(2)
    own_head = (
        lax.broadcasted_iota(jnp.int32, (HEADS * CP, D), 0) // CP
        == lax.broadcasted_iota(jnp.int32, (HEADS * CP, D), 1) // HD
    )
    scale = math.log2(math.e) / math.sqrt(HD)
    one_row = (lax.broadcasted_iota(jnp.int32, (16, 64), 0) == 0).astype(F32)
    one_row_all = (lax.broadcasted_iota(jnp.int32, (16, 1024), 0) == 0).astype(F32)
    for frame in range(2):
        query_part = query_all[32 * frame : 32 * (frame + 1)]
        key_part = key_all[32 * frame : 32 * (frame + 1)]
        value_part = value_all[32 * frame : 32 * (frame + 1)]
        key_heads = jnp.where(own_head, jnp.concatenate([key_part] * HEADS, axis=0), 0.0).astype(BF)
        pair = dot_nt(key_heads, query_part.astype(BF)) * scale
        own = jnp.concatenate([own_ref[0, 0:16, 64 * frame : 64 * (frame + 1)], one_row], axis=0)
        own_high, own_low = split(own)
        pair_high, pair_low = split(pair)
        reduced = dot_nn(
            jnp.concatenate([pair_high, pair_low, pair_high], axis=1),
            jnp.concatenate([own_high, own_high, own_low], axis=0),
        )
        for head in range(HEADS):
            query_ref[:, 64 * head : 64 * (head + 1)] = reduced[CP * head : CP * (head + 1)]
        query_high, query_low = split(query_ref[...])
        queries = jnp.concatenate([query_high, query_low, query_high], axis=0)
        tokens = tokens_ref[frame]
        token_high, token_low = split(jnp.concatenate([tokens, one_row_all], axis=0))
        keys = jnp.concatenate([token_high, token_high, token_low], axis=0)
        values = jnp.concatenate(
            [token_high, token_low[0:16]], axis=0
        )
        for chunk in range(4):
            scores = dot_tn(keys, queries[:, 256 * chunk : 256 * (chunk + 1)])
            top = jnp.max(scores, axis=0, keepdims=True)
            weights = jnp.exp2(scores - top).astype(BF)
            summed = dot_nn(values, weights)
            mixed = (summed[0:16] + summed[32:48]) / summed[16:17]
            for sub in range(4):
                head = 4 * chunk + sub
                part_ref[frame, CP * head : CP * head + 16, :] = mixed[:, 64 * sub : 64 * (sub + 1)]
                part_ref[frame, CP * head + 16 : CP * head + 32, :] = one_row
        value_heads = jnp.where(own_head, jnp.concatenate([value_part] * HEADS, axis=0), 0.0).astype(BF)
        mix_ref[64 * frame : 64 * (frame + 1), :] = dot_tn(
            part_ref[frame].astype(BF), value_heads
        ).astype(BF)


def chip_order(me):
    across = me ^ 2
    return [
        me,
        across,
        lax.rem(me + 12, 16),
        lax.rem(me + 4, 16),
        lax.rem(across + 12, 16),
        lax.rem(across + 4, 16),
        lax.rem(me + 8, 16),
        lax.rem(across + 8, 16),
    ]


def at_rows(index):
    return pl.ds(pl.multiple_of(index * HD, 8), HD)


def hidden_kernel(mix_ref, latents_ref, embed_ref, mod_ref, *rest):
    *blocks, hidden_ref, inner_ref, update_ref = rest
    order = chip_order(lax.axis_index("seq"))
    mix = mix_ref[...]
    for place, index in enumerate(order):
        update_ref[at_rows(index), :] = dot_nt(blocks[0][place], mix)
        update_ref[at_rows(index ^ 1), :] = dot_nt(blocks[1][place], mix)
    embedded = product_tn(embed_ref[...], both_frames(latents_ref))
    gate, shift, scale = modulation_columns(mod_ref[...], (2, 3, 4))
    hidden = embedded + gate * update_ref[...]
    hidden_ref[...] = hidden
    inner_ref[...] = (normalize(hidden) * (1.0 + scale) + shift).astype(BF)


def temporal_kernel(advance_ref, own_ref, peer_ref, own_next_ref, peer_next_ref, *rest):
    *blocks, out_own_ref, out_peer_ref = rest
    tokens = jnp.concatenate([own_ref[...], peer_ref[...]], axis=1)
    following = jnp.concatenate([own_next_ref[...], peer_next_ref[...]], axis=1)
    last = lax.axis_index("queue") == lax.axis_size("queue") - 1
    limit = jnp.where(last, 0, advance_ref[0])
    frame = lax.broadcasted_iota(jnp.int32, (1, 128), 1) // 64
    keep_same = frame < limit
    keep_other = (1 - frame) < limit
    scale = math.log2(math.e) / math.sqrt(HD)
    for place, block in enumerate(blocks):
        query = dot_nn(block[0], tokens) * scale
        key = dot_nn(block[1], tokens)
        key_next = dot_nn(block[1], following)
        value = dot_nn(block[2], tokens)
        value_next = dot_nn(block[2], following)
        for side, out_ref in enumerate((out_own_ref, out_peer_ref)):
            lanes = slice(128 * side, 128 * (side + 1))
            asked = query[:, lanes]
            keys = [key[:, lanes], key_next[:, lanes]]
            values = [value[:, lanes], value_next[:, lanes]]
            keys = [keys[0], pltpu.roll(keys[0], 64, 1), keys[1], pltpu.roll(keys[1], 64, 1)]
            values = [values[0], pltpu.roll(values[0], 64, 1), values[1], pltpu.roll(values[1], 64, 1)]
            scores = [jnp.sum(asked * one, axis=0, keepdims=True) for one in keys]
            scores[2] = jnp.where(keep_same, scores[2], -1e30)
            scores[3] = jnp.where(keep_other, scores[3], -1e30)
            top = jnp.maximum(jnp.maximum(scores[0], scores[1]), jnp.maximum(scores[2], scores[3]))
            weights = [jnp.exp2(one - top) for one in scores]
            inverse = 1.0 / (weights[0] + weights[1] + weights[2] + weights[3])
            mixed = sum(w * inverse * v for w, v in zip(weights, values))
            out_ref[HD * place : HD * (place + 1), :] = mixed


def final_kernel(own_ref, peer_ref, hidden_ref, latents_ref, mod_ref, final_ref, *rest):
    *blocks, velocity_ref, updated_ref, mix_ref, update_ref = rest
    order = chip_order(lax.axis_index("seq"))
    for place, index in enumerate(order):
        rows = slice(HD * place, HD * (place + 1))
        mix_ref[at_rows(index), :] = own_ref[rows, :].astype(F32)
        mix_ref[at_rows(index ^ 1), :] = peer_ref[rows, :].astype(F32)
    mix = mix_ref[...].astype(BF)
    for place, index in enumerate(order):
        update_ref[at_rows(index), :] = dot_nn(blocks[0][place], mix)
        update_ref[at_rows(index ^ 1), :] = dot_nn(blocks[1][place], mix)
    gate, shift, scale = modulation_columns(mod_ref[...], (5, 6, 7))
    hidden = hidden_ref[...] + gate * update_ref[...]
    inner = (normalize(hidden) * (1.0 + scale) + shift).astype(BF)
    velocity = dot_nn(final_ref[...], inner)
    for frame in range(2):
        part = velocity[:, 64 * frame : 64 * (frame + 1)]
        velocity_ref[frame] = part
        updated_ref[frame] = latents_ref[frame] - part * (1.0 / 32.0)


def params(mebibytes):
    return pltpu.CompilerParams(vmem_limit_bytes=mebibytes << 20)


def cost(flops, moved):
    return pl.CostEstimate(flops=flops, bytes_accessed=moved, transcendentals=0)


def along_seq(array, to):
    return lax.ppermute(array, "seq", [(i, to(i)) for i in range(16)])


def y_up(array):
    return along_seq(array, lambda i: (i + 4) % 16)


def y_down(array):
    return along_seq(array, lambda i: (i + 12) % 16)


def over_x(array):
    return along_seq(array, lambda i: i ^ 2)


def other_core(array):
    return along_seq(array, lambda i: i ^ 1)


def from_next(array):
    return lax.ppermute(array, "queue", [(i, i - 1) for i in range(1, 16)])


def gather(own):
    across = over_x(own)
    below, above = y_up(own), y_down(own)
    below_across, above_across = y_up(across), y_down(across)
    return [own, across, below, above, below_across, above_across, y_up(below), y_down(above_across)]


def shards(
    latents,
    levels,
    advance,
    fresh_noise,
    level_mod,
    embed_w,
    spatial_qkv,
    spatial_out,
    temporal_qkv,
    temporal_out,
    final_w,
):
    lat = latents.transpose(0, 2, 1)
    spatial_w = spatial_qkv.transpose(1, 0, 2)
    out_w = spatial_out.transpose(1, 0)
    temporal_w = temporal_qkv.transpose(1, 2, 0)
    last_w = temporal_out.transpose(1, 0)
    final_t = final_w.transpose(1, 0)

    packed = pl.pallas_call(
        pack_kernel,
        out_shape=jax.ShapeDtypeStruct((16, 32, 128), F32),
        in_specs=[SMEM, VMEM, VMEM, VMEM],
        out_specs=VMEM,
        name="pack",
    )(levels, lat, embed_w, level_mod)
    everyone = lax.all_to_all(packed, "seq", split_axis=0, concat_axis=0, tiled=True)
    out_own = jnp.stack(gather(out_w))
    out_peer = other_core(out_own)
    temporal_blocks = gather(temporal_w)
    last_own = jnp.stack(gather(last_w))
    last_peer = other_core(last_own)

    mix, mod = pl.pallas_call(
        spatial_kernel,
        out_shape=(
            jax.ShapeDtypeStruct((128, D), BF),
            jax.ShapeDtypeStruct((16, D), F32),
        ),
        in_specs=[VMEM] * 4,
        out_specs=(VMEM, VMEM),
        scratch_shapes=[
            pltpu.VMEM((2, 16, 1024), F32),
            pltpu.VMEM((CP, 1024), F32),
            pltpu.VMEM((2, HEADS * CP, 64), F32),
        ],
        compiler_params=params(40),
        cost_estimate=cost(10**10, 10**7),
        name="spatial",
    )(packed, everyone, embed_w, spatial_w)

    hidden, inner = pl.pallas_call(
        hidden_kernel,
        out_shape=(
            jax.ShapeDtypeStruct((D, 128), F32),
            jax.ShapeDtypeStruct((D, 128), BF),
        ),
        in_specs=[VMEM] * 6,
        out_specs=(VMEM, VMEM),
        scratch_shapes=[pltpu.VMEM((D, 128), F32)],
        compiler_params=params(32),
        name="hidden",
    )(mix, lat, embed_w, mod, out_own, out_peer)
    following = from_next(inner)
    inner_peer = other_core(inner)
    following_peer = other_core(following)
    parts = []
    for first, end in ((0, 4), (4, 6), (6, 8)):
        rows = HD * (end - first)
        parts.append(
            pl.pallas_call(
                temporal_kernel,
                out_shape=(
                    jax.ShapeDtypeStruct((rows, 128), F32),
                    jax.ShapeDtypeStruct((rows, 128), F32),
                ),
                in_specs=[SMEM] + [VMEM] * (4 + end - first),
                out_specs=(VMEM, VMEM),
                compiler_params=params(32),
                name=f"temporal_{first}",
            )(advance, inner, inner_peer, following, following_peer, *temporal_blocks[first:end])
        )
    mix_own = jnp.concatenate([part[0] for part in parts], axis=0)
    mix_peer = jnp.concatenate([other_core(part[1].astype(BF)) for part in parts], axis=0)
    velocity, updated = pl.pallas_call(
        final_kernel,
        out_shape=(
            jax.ShapeDtypeStruct((2, C, 64), F32),
            jax.ShapeDtypeStruct((2, C, 64), F32),
        ),
        in_specs=[VMEM] * 8,
        out_specs=(VMEM, VMEM),
        scratch_shapes=[pltpu.VMEM((D, 128), F32), pltpu.VMEM((D, 128), F32)],
        compiler_params=params(32),
        name="final",
    )(mix_own, mix_peer, hidden, lat, mod, final_t, last_own, last_peer)
    incoming = from_next(updated[0])
    is_last = lax.axis_index("queue") == lax.axis_size("queue") - 1
    tail = jnp.where(is_last, fresh_noise.transpose(1, 0), incoming)
    queue_next = jnp.stack([updated[1], tail])
    return velocity.transpose(0, 2, 1), queue_next.transpose(0, 2, 1)


def solution(mesh):
    placed = (
        P("queue", "seq", None),
        P("queue"),
        P("queue"),
        P("seq", None),
        P(None, None, "seq"),
        P(),
        P(),
        P(None, "seq"),
        P(None, None, "seq"),
        P(None, "seq"),
        P(),
    )
    return jax.shard_map(
        shards,
        mesh=mesh,
        in_specs=placed,
        out_specs=(P("queue", "seq", None), P("queue", "seq", None)),
        check_vma=False,
    )
```

```python
import functools
import math

import jax
import jax.numpy as jnp
from jax import lax
from jax.experimental import pallas as pl
from jax.experimental.pallas import tpu as pltpu
from jax.sharding import PartitionSpec as P

HEADS = 16
HD = 72
D = HEADS * HD
C = 16
CP = 32
BF = jnp.bfloat16
F32 = jnp.float32
VMEM = pl.BlockSpec(memory_space=pltpu.VMEM)
SMEM = pl.BlockSpec(memory_space=pltpu.SMEM)
ANY = pl.BlockSpec(memory_space=pl.ANY)


def split(value):
    high = value.astype(BF)
    return high, (value - high.astype(F32)).astype(BF)


def dot_tn(a, b):
    return lax.dot_general(a, b, (((0,), (0,)), ((), ())), preferred_element_type=F32)


def dot_nt(a, b):
    return lax.dot_general(a, b, (((1,), (1,)), ((), ())), preferred_element_type=F32)


def dot_nn(a, b):
    return jnp.dot(a, b, preferred_element_type=F32)


def product_tn(a, b):
    a_high, a_low = split(a)
    b_high, b_low = split(b)
    return dot_tn(
        jnp.concatenate([a_high, a_low, a_high], axis=0),
        jnp.concatenate([b_high, b_high, b_low], axis=0),
    )


def both_frames(latents_ref):
    return jnp.concatenate([latents_ref[0], latents_ref[1]], axis=1)


def normalize(hidden):
    width = hidden.shape[0]
    mean_value = jnp.sum(hidden, axis=0, keepdims=True) * (1.0 / width)
    centered = hidden - mean_value
    variance = jnp.sum(centered * centered, axis=0, keepdims=True) * (1.0 / width)
    return centered * lax.rsqrt(variance + 1e-06)


def modulation_columns(mod, rows):
    tokens = 128
    high, low = split(mod)
    row_at = lax.broadcasted_iota(jnp.int32, (16, tokens * len(rows)), 0)
    lane_at = lax.broadcasted_iota(jnp.int32, (16, tokens * len(rows)), 1)
    wanted = jnp.zeros_like(row_at)
    for place, row in enumerate(rows):
        wanted = jnp.where(lane_at // tokens == place, row, wanted)
    wanted = wanted + 8 * ((lane_at % tokens) // 64)
    chosen = (row_at == wanted).astype(F32).astype(BF)
    columns = dot_tn(
        jnp.concatenate([high, low], axis=0), jnp.concatenate([chosen, chosen], axis=0)
    )
    return [columns[:, tokens * i : tokens * (i + 1)] for i in range(len(rows))]


def pack_kernel(levels_ref, latents_ref, embed_ref, table_ref, out_ref):
    channels = both_frames(latents_ref)
    embed = embed_ref[...]
    centered = embed - jnp.sum(embed, axis=1, keepdims=True) * (1.0 / D)
    spread = product_tn(centered, channels)
    variance = jnp.sum(spread * spread, axis=0, keepdims=True) * (1.0 / D)
    inverse = lax.rsqrt(variance + 1e-06)
    peers = out_ref.shape[0]
    for peer in range(peers):
        out_ref[peer, 0:16, :] = channels
        out_ref[peer, 32:40, :] = jnp.broadcast_to(inverse, (8, 128))
        for frame in range(2):
            rows = table_ref[levels_ref[frame]]
            out_ref[peer, 16 + 8 * frame : 24 + 8 * frame, 0:HD] = rows


def coefficient_kernel(all_ref, embed_ref, weight_ref, coef_ref, mod_ref, tokens_ref, held_ref, sems):
    parts, rows = sems.shape[1], D // sems.shape[1]
    copies = [
        [
            pltpu.make_async_copy(
                weight_ref.at[index, pl.ds(rows * part, rows)],
                held_ref.at[index, pl.ds(rows * part, rows)],
                sems.at[index, part],
            )
            for part in range(parts)
        ]
        for index in range(3)
    ]
    for index in range(3):
        for copy in copies[index]:
            copy.start()
    peers = all_ref.shape[0]
    for peer in range(peers):
        mod_ref[:, HD * peer : HD * (peer + 1)] = all_ref[peer, 16:32, 0:HD]
        scaled = all_ref[peer, 0:16] * all_ref[peer, 32:33]
        for frame in range(2):
            tokens_ref[frame, :, 64 * peer : 64 * (peer + 1)] = scaled[:, 64 * frame : 64 * (frame + 1)]
    mod = mod_ref[...]
    embed = embed_ref[...]
    centered = embed - jnp.sum(embed, axis=1, keepdims=True) * (1.0 / D)
    row16 = lax.broadcasted_iota(jnp.int32, (16, D), 0)
    rows = []
    for frame in range(2):
        rows.append(centered * (1.0 + mod[8 * frame + 1 : 8 * frame + 2]))
        rows.append(jnp.where(row16 == 0, mod[8 * frame : 8 * frame + 1], 0.0))
    high, low = split(jnp.concatenate(rows, axis=0))
    stacked = jnp.concatenate([high, low], axis=0)
    for index in range(3):
        for copy in copies[index]:
            copy.wait()
        both = dot_nn(stacked, held_ref[index])
        for frame in range(2):
            rows = slice(CP * frame, CP * (frame + 1))
            coef_ref[frame, index] = both[rows] + both[64:128][rows]


def attend_kernel(frame, own_ref, tokens_ref, coef_ref, *refs):
    mix_ref, query_ref, part_ref = refs[-3:]
    own_head = (
        lax.broadcasted_iota(jnp.int32, (HEADS * CP, D), 0) // CP
        == lax.broadcasted_iota(jnp.int32, (HEADS * CP, D), 1) // HD
    )
    scale = math.log2(math.e) / math.sqrt(HD)
    one_row = (lax.broadcasted_iota(jnp.int32, (16, 64), 0) == 0).astype(F32)
    one_row_all = (lax.broadcasted_iota(jnp.int32, (16, 1024), 0) == 0).astype(F32)
    key_heads = jnp.where(own_head, jnp.concatenate([coef_ref[frame, 1]] * HEADS, axis=0), 0.0).astype(BF)
    pair = dot_nt(key_heads, coef_ref[frame, 0].astype(BF)) * scale
    mine = own_ref[0:16] * own_ref[32:33]
    own = jnp.concatenate([mine[:, 64 * frame : 64 * (frame + 1)], one_row], axis=0)
    own_high, own_low = split(own)
    pair_high, pair_low = split(pair)
    reduced = dot_nn(
        jnp.concatenate([pair_high, pair_low, pair_high], axis=1),
        jnp.concatenate([own_high, own_high, own_low], axis=0),
    )
    for head in range(HEADS):
        query_ref[:, 64 * head : 64 * (head + 1)] = reduced[CP * head : CP * (head + 1)]
    query_high, query_low = split(query_ref[...])
    queries = jnp.concatenate([query_high, query_low, query_high], axis=0)
    token_high, token_low = split(jnp.concatenate([tokens_ref[frame], one_row_all], axis=0))
    keys = jnp.concatenate([token_high, token_high, token_low], axis=0)
    values = jnp.concatenate([token_high, token_low[0:16]], axis=0)
    for chunk in range(4):
        scores = dot_tn(keys, queries[:, 256 * chunk : 256 * (chunk + 1)])
        top = jnp.max(scores, axis=0, keepdims=True)
        weights = jnp.exp2(scores - top).astype(BF)
        summed = dot_nn(values, weights)
        mixed = (summed[0:16] + summed[32:48]) / summed[16:17]
        for sub in range(4):
            head = 4 * chunk + sub
            part_ref[CP * head : CP * head + 16, :] = mixed[:, 64 * sub : 64 * (sub + 1)]
            part_ref[CP * head + 16 : CP * head + 32, :] = one_row
    value_heads = jnp.where(own_head, jnp.concatenate([coef_ref[frame, 2]] * HEADS, axis=0), 0.0).astype(BF)
    mix_ref[...] = dot_tn(part_ref[...].astype(BF), value_heads).astype(BF)


def lay_kernel(after_ref, source_ref, out_ref):
    out_ref[...] = source_ref[...]


def gate_kernel(after_ref, held_ref, passed_ref):
    pass


def y_order(me):
    return [me, lax.rem(me + 12, 16), lax.rem(me + 4, 16), lax.rem(me + 8, 16)]


def at_rows(index):
    return pl.ds(pl.multiple_of(index * HD, 8), HD)


def place_rows(out_ref, product, order):
    for place, index in enumerate(order):
        out_ref[at_rows(index), :] = product[HD * place : HD * (place + 1)]


def hidden_kernel(first_ref, second_ref, latents_ref, embed_ref, mod_ref, *rest):
    *blocks, hidden_ref, inner_ref, update_ref = rest
    mix = jnp.concatenate([first_ref[...], second_ref[...]], axis=0).T
    me = lax.axis_index("seq")
    for flip, block in enumerate(blocks):
        place_rows(update_ref, dot_nn(block[...], mix), y_order(me ^ flip))
    embedded = product_tn(embed_ref[...], both_frames(latents_ref))
    gate, shift, scale = modulation_columns(mod_ref[...], (2, 3, 4))
    hidden = embedded + gate * update_ref[...]
    hidden_ref[...] = hidden
    inner_ref[...] = (normalize(hidden) * (1.0 + scale) + shift).astype(BF)


def temporal_kernel(advance_ref, *refs):
    sources, outs, (held_ref, sems) = refs[:4], refs[12:16], refs[16:]
    copies = [
        pltpu.make_async_copy(source, held_ref.at[place], sems.at[place]) for place, source in enumerate(sources)
    ]
    for copy in copies:
        copy.start()
    tokens = jnp.concatenate([one[...] for one in refs[4:8]], axis=1)
    following = jnp.concatenate([one[...] for one in refs[8:12]], axis=1)
    last = lax.axis_index("queue") == lax.axis_size("queue") - 1
    limit = jnp.where(last, 0, advance_ref[0])
    frame = lax.broadcasted_iota(jnp.int32, (1, 128), 1) // 64
    keep_same = frame < limit
    keep_other = (1 - frame) < limit
    scale = math.log2(math.e) / math.sqrt(HD)
    for place, copy in enumerate(copies):
        copy.wait()
        block = held_ref[place]
        both = dot_nn(block, tokens)
        ahead = dot_nn(block[HD : 3 * HD], following)
        query, key, value = (both[HD * index : HD * (index + 1)] for index in range(3))
        key_next, value_next = ahead[0:HD], ahead[HD : 2 * HD]
        for side, out_ref in enumerate(outs):
            lanes = slice(128 * side, 128 * (side + 1))
            asked = query[:, lanes] * scale
            keys = [key[:, lanes], key_next[:, lanes]]
            values = [value[:, lanes], value_next[:, lanes]]
            keys = [keys[0], pltpu.roll(keys[0], 64, 1), keys[1], pltpu.roll(keys[1], 64, 1)]
            values = [values[0], pltpu.roll(values[0], 64, 1), values[1], pltpu.roll(values[1], 64, 1)]
            scores = [jnp.sum(asked * one, axis=0, keepdims=True) for one in keys]
            scores[2] = jnp.where(keep_same, scores[2], -1e30)
            scores[3] = jnp.where(keep_other, scores[3], -1e30)
            top = jnp.maximum(jnp.maximum(scores[0], scores[1]), jnp.maximum(scores[2], scores[3]))
            weights = [jnp.exp2(one - top) for one in scores]
            inverse = 1.0 / (weights[0] + weights[1] + weights[2] + weights[3])
            mixed = sum(w * inverse * v for w, v in zip(weights, values))
            out_ref[HD * place : HD * (place + 1), :] = mixed.astype(BF)


def final_kernel(hidden_ref, latents_ref, mod_ref, final_ref, *rest):
    mixes, blocks, (velocity_ref, updated_ref, mix_ref, update_ref) = rest[0:4], rest[4:6], rest[6:]
    me = lax.axis_index("seq")
    for flip, part in enumerate(mixes):
        place_rows(mix_ref, part[...].astype(F32), y_order(me ^ flip))
    mix = mix_ref[...].astype(BF)
    for flip, block in enumerate(blocks):
        at = lax.rem(me ^ flip, 4)
        order = [4 * place + (at ^ side) for place in range(4) for side in (0, 2)]
        place_rows(update_ref, dot_nn(block[...], mix), order)
    gate, shift, scale = modulation_columns(mod_ref[...], (5, 6, 7))
    hidden = hidden_ref[...] + gate * update_ref[...]
    inner = (normalize(hidden) * (1.0 + scale) + shift).astype(BF)
    velocity = dot_nn(final_ref[...], inner)
    for frame in range(2):
        part = velocity[:, 64 * frame : 64 * (frame + 1)]
        velocity_ref[frame] = part
        updated_ref[frame] = latents_ref[frame] - part * (1.0 / 32.0)


def params(mebibytes):
    return pltpu.CompilerParams(vmem_limit_bytes=mebibytes << 20)


def takes(microseconds):
    return pl.CostEstimate(
        flops=int(microseconds * 1.15e9), bytes_accessed=1000, transcendentals=0
    )


def along_seq(array, to):
    return lax.ppermute(array, "seq", [(i, to(i)) for i in range(16)])


def y_up(array):
    return along_seq(array, lambda i: (i + 4) % 16)


def y_down(array):
    return along_seq(array, lambda i: (i + 12) % 16)


def over_x(array):
    return along_seq(array, lambda i: i ^ 2)


def other_core(array):
    return along_seq(array, lambda i: i ^ 1)


def from_next(array):
    return lax.ppermute(array, "queue", [(i, i - 1) for i in range(1, 16)])


def over_both(array):
    return along_seq(array, lambda i: i ^ 3)


def y_far(array):
    return along_seq(array, lambda i: (i + 8) % 16)


def stack_after(after, blocks, name):
    return pl.pallas_call(
        stack_kernel,
        out_shape=jax.ShapeDtypeStruct((len(blocks), *blocks[0].shape), BF),
        in_specs=[VMEM] * (1 + len(blocks)),
        out_specs=VMEM,
        cost_estimate=takes(2),
        name=name,
    )(after, *blocks)


def gate(held, after, name):
    return pl.pallas_call(
        gate_kernel,
        out_shape=jax.ShapeDtypeStruct(held.shape, held.dtype),
        in_specs=[ANY, ANY],
        out_specs=ANY,
        input_output_aliases={1: 0},
        cost_estimate=takes(0.2),
        name=name,
    )(after, held)


def shards(
    latents,
    levels,
    advance,
    fresh_noise,
    level_mod,
    embed_w,
    spatial_qkv,
    spatial_out,
    temporal_qkv,
    temporal_out,
    final_w,
):
    lat = latents.transpose(0, 2, 1)
    spatial_w = spatial_qkv.transpose(1, 0, 2)
    out_w = spatial_out.transpose(1, 0)
    temporal_w = temporal_qkv.transpose(1, 2, 0).reshape(3 * HD, D)
    last_w = temporal_out.transpose(1, 0)
    final_t = final_w.transpose(1, 0)

    packed = pl.pallas_call(
        pack_kernel,
        out_shape=jax.ShapeDtypeStruct((16, 40, 128), F32),
        in_specs=[SMEM, VMEM, VMEM, VMEM],
        out_specs=VMEM,
        cost_estimate=takes(2),
        name="pack",
    )(levels, lat, embed_w, level_mod)
    everyone = lax.all_to_all(packed, "seq", split_axis=0, concat_axis=0, tiled=True)
    with jax.named_scope("out_y"):
        out_own = jnp.stack([out_w, y_up(out_w), y_down(out_w), y_far(out_w)])
    with jax.named_scope("out_x"):
        out_across = over_x(out_own)
    with jax.named_scope("out_core"):
        out_peer = other_core(out_own)
    qkv_copy = pl.pallas_call(
        lay_kernel,
        out_shape=jax.ShapeDtypeStruct((3 * HD, D), BF),
        in_specs=[ANY, VMEM],
        out_specs=VMEM,
        cost_estimate=takes(1.5),
        name="lay",
    )(out_own, temporal_w)
    with jax.named_scope("qkv_y"):
        below, above, far = y_up(qkv_copy), y_down(qkv_copy), y_far(qkv_copy)
    with jax.named_scope("last_x"):
        last_pair = jnp.stack([last_w, over_x(last_w)])
    last_held = gate(last_pair, far, "gate_pair")
    with jax.named_scope("last_y"):
        rings = [[4 * y + i for y in range(4)] for i in range(4)]
        last_own = lax.all_to_all(
            jnp.broadcast_to(last_held[None], (4, 2, HD, D)),
            "seq",
            split_axis=0,
            concat_axis=0,
            tiled=True,
            axis_index_groups=rings,
        )

    coef, mod, tokens = pl.pallas_call(
        coefficient_kernel,
        out_shape=(
            jax.ShapeDtypeStruct((2, 3, CP, D), F32),
            jax.ShapeDtypeStruct((16, D), F32),
            jax.ShapeDtypeStruct((2, 16, 1024), F32),
        ),
        in_specs=[VMEM] * 2 + [ANY],
        out_specs=(VMEM, VMEM, VMEM),
        scratch_shapes=[pltpu.VMEM((3, D, D), BF), pltpu.SemaphoreType.DMA((3, 4))],
        compiler_params=params(48),
        cost_estimate=takes(20),
        name="coefficients",
    )(everyone, embed_w, spatial_w)

    def attend(frame, *after):
        return pl.pallas_call(
            functools.partial(attend_kernel, frame),
            out_shape=jax.ShapeDtypeStruct((64, D), BF),
            in_specs=[VMEM] * 3 + [ANY] * len(after),
            out_specs=VMEM,
            scratch_shapes=[
                pltpu.VMEM((CP, 1024), F32),
                pltpu.VMEM((HEADS * CP, 64), F32),
            ],
            compiler_params=params(24),
            cost_estimate=takes(1),
            name="attend",
        )(packed[0], tokens, coef, *after)

    first = attend(0)
    second = attend(1, first, below, above, last_pair)
    out_across = gate(out_across, second, "gate_out")
    with jax.named_scope("out_core"):
        out_both = other_core(out_across)

    hidden, inner = pl.pallas_call(
        hidden_kernel,
        out_shape=(
            jax.ShapeDtypeStruct((D, 128), F32),
            jax.ShapeDtypeStruct((D, 128), BF),
        ),
        in_specs=[VMEM] * 9,
        out_specs=(VMEM, VMEM),
        scratch_shapes=[pltpu.VMEM((D, 128), F32)],
        compiler_params=params(24),
        cost_estimate=takes(2),
        name="hidden",
    )(first, second, lat, embed_w, mod, *(one.reshape(4 * HD, D) for one in (out_own, out_peer, out_across, out_both)))
    with jax.named_scope("inner"):
        pairs = [(16 * q + j, 16 * (q - 1) + (j ^ 2)) for q in range(1, 16) for j in range(16)]
        following_across = lax.ppermute(inner, ("queue", "seq"), pairs)
        across = over_x(inner)
        following = from_next(inner)
    with jax.named_scope("inner_core"):
        tokens_four = [inner, other_core(inner), across, other_core(across)]
        following_four = [following, other_core(following), following_across, other_core(following_across)]
    parts = pl.pallas_call(
        temporal_kernel,
        out_shape=(jax.ShapeDtypeStruct((4 * HD, 128), BF),) * 4,
        in_specs=[SMEM] + [ANY] * 4 + [VMEM] * 8,
        out_specs=(VMEM,) * 4,
        scratch_shapes=[pltpu.VMEM((4, 3 * HD, D), BF), pltpu.SemaphoreType.DMA((4,))],
        compiler_params=params(48),
        cost_estimate=takes(4),
        name="temporal",
    )(advance, qkv_copy, below, above, far, *tokens_four, *following_four)
    last_own = gate(last_own, parts[0], "gate_last")
    with jax.named_scope("last_core"):
        last_all = [one.reshape(8 * HD, D) for one in (last_own, other_core(last_own))]
    with jax.named_scope("back"):
        mix_all = [parts[0], other_core(parts[1]), over_x(parts[2]), over_both(parts[3])]
    velocity, updated = pl.pallas_call(
        final_kernel,
        out_shape=(
            jax.ShapeDtypeStruct((2, C, 64), F32),
            jax.ShapeDtypeStruct((2, C, 64), F32),
        ),
        in_specs=[VMEM] * 10,
        out_specs=(VMEM, VMEM),
        scratch_shapes=[pltpu.VMEM((D, 128), F32), pltpu.VMEM((D, 128), F32)],
        compiler_params=params(24),
        cost_estimate=takes(2.4),
        name="final",
    )(hidden, lat, mod, final_t, *mix_all, *last_all)
    incoming = from_next(updated[0])
    is_last = lax.axis_index("queue") == lax.axis_size("queue") - 1
    tail = jnp.where(is_last, fresh_noise.transpose(1, 0), incoming)
    queue_next = jnp.stack([updated[1], tail])
    return velocity.transpose(0, 2, 1), queue_next.transpose(0, 2, 1)


def solution(mesh):
    placed = (
        P("queue", "seq", None),
        P("queue"),
        P("queue"),
        P("seq", None),
        P(None, None, "seq"),
        P(),
        P(),
        P(None, "seq"),
        P(None, None, "seq"),
        P(None, "seq"),
        P(),
    )
    return jax.shard_map(
        shards,
        mesh=mesh,
        in_specs=placed,
        out_specs=(P("queue", "seq", None), P("queue", "seq", None)),
        check_vma=False,
    )
```

```python
import functools
import math

import jax
import jax.numpy as jnp
from jax import lax
from jax.experimental import pallas as pl
from jax.experimental.pallas import tpu as pltpu
from jax.sharding import PartitionSpec as P

HEADS = 16
HD = 72
D = HEADS * HD
C = 16
CP = 32
BF = jnp.bfloat16
F32 = jnp.float32
VMEM = pl.BlockSpec(memory_space=pltpu.VMEM)
SMEM = pl.BlockSpec(memory_space=pltpu.SMEM)
ANY = pl.BlockSpec(memory_space=pl.ANY)


def split(value):
    high = value.astype(BF)
    return high, (value - high.astype(F32)).astype(BF)


def dot_tn(a, b):
    return lax.dot_general(a, b, (((0,), (0,)), ((), ())), preferred_element_type=F32)


def dot_nt(a, b):
    return lax.dot_general(a, b, (((1,), (1,)), ((), ())), preferred_element_type=F32)


def dot_nn(a, b):
    return jnp.dot(a, b, preferred_element_type=F32)


def product_tn(a, b):
    a_high, a_low = split(a)
    b_high, b_low = split(b)
    return dot_tn(
        jnp.concatenate([a_high, a_low, a_high], axis=0),
        jnp.concatenate([b_high, b_high, b_low], axis=0),
    )


def both_frames(latents_ref):
    return jnp.concatenate([latents_ref[0], latents_ref[1]], axis=1)


def normalize(hidden):
    width = hidden.shape[0]
    mean_value = jnp.sum(hidden, axis=0, keepdims=True) * (1.0 / width)
    centered = hidden - mean_value
    variance = jnp.sum(centered * centered, axis=0, keepdims=True) * (1.0 / width)
    return centered * lax.rsqrt(variance + 1e-06)


def modulation_columns(mod, rows):
    tokens = 128
    high, low = split(mod)
    row_at = lax.broadcasted_iota(jnp.int32, (16, tokens * len(rows)), 0)
    lane_at = lax.broadcasted_iota(jnp.int32, (16, tokens * len(rows)), 1)
    wanted = jnp.zeros_like(row_at)
    for place, row in enumerate(rows):
        wanted = jnp.where(lane_at // tokens == place, row, wanted)
    wanted = wanted + 8 * ((lane_at % tokens) // 64)
    chosen = (row_at == wanted).astype(F32).astype(BF)
    columns = dot_tn(
        jnp.concatenate([high, low], axis=0), jnp.concatenate([chosen, chosen], axis=0)
    )
    return [columns[:, tokens * i : tokens * (i + 1)] for i in range(len(rows))]


def pack_kernel(levels_ref, latents_ref, embed_ref, table_ref, after_ref, out_ref, own_ref):
    channels = both_frames(latents_ref)
    embed = embed_ref[...]
    centered = embed - jnp.sum(embed, axis=1, keepdims=True) * (1.0 / D)
    spread = product_tn(centered, channels)
    variance = jnp.sum(spread * spread, axis=0, keepdims=True) * (1.0 / D)
    inverse = lax.rsqrt(variance + 1e-06)
    own_ref[...] = channels * inverse
    peers = out_ref.shape[0]
    for peer in range(peers):
        out_ref[peer, 0:16, :] = channels
        out_ref[peer, 32:40, :] = jnp.broadcast_to(inverse, (8, 128))
        for frame in range(2):
            rows = table_ref[levels_ref[frame]]
            out_ref[peer, 16 + 8 * frame : 24 + 8 * frame, 0:HD] = rows


def coefficient_kernel(all_ref, embed_ref, weight_ref, coef_ref, mod_ref, tokens_ref, held_ref, sems):
    parts, rows = sems.shape[1], D // sems.shape[1]
    copies = [
        [
            pltpu.make_async_copy(
                weight_ref.at[index, pl.ds(rows * part, rows)],
                held_ref.at[index, pl.ds(rows * part, rows)],
                sems.at[index, part],
            )
            for part in range(parts)
        ]
        for index in range(3)
    ]
    for index in range(3):
        for copy in copies[index]:
            copy.start()
    peers = all_ref.shape[0]
    for peer in range(peers):
        mod_ref[:, HD * peer : HD * (peer + 1)] = all_ref[peer, 16:32, 0:HD]
        scaled = all_ref[peer, 0:16] * all_ref[peer, 32:33]
        for frame in range(2):
            tokens_ref[frame, :, 64 * peer : 64 * (peer + 1)] = scaled[:, 64 * frame : 64 * (frame + 1)]
    mod = mod_ref[...]
    embed = embed_ref[...]
    centered = embed - jnp.sum(embed, axis=1, keepdims=True) * (1.0 / D)
    row16 = lax.broadcasted_iota(jnp.int32, (16, D), 0)
    rows = []
    for frame in range(2):
        rows.append(centered * (1.0 + mod[8 * frame + 1 : 8 * frame + 2]))
        rows.append(jnp.where(row16 == 0, mod[8 * frame : 8 * frame + 1], 0.0))
    high, low = split(jnp.concatenate(rows, axis=0))
    stacked = jnp.concatenate([high, low], axis=0)
    for index in range(3):
        for copy in copies[index]:
            copy.wait()
        both = dot_nn(stacked, held_ref[index])
        for frame in range(2):
            rows = slice(CP * frame, CP * (frame + 1))
            coef_ref[frame, index] = both[rows] + both[64:128][rows]


def attend_kernel(frame, own_ref, tokens_ref, coef_ref, *refs):
    mix_ref, query_ref, part_ref = refs[-3:]
    own_head = (
        lax.broadcasted_iota(jnp.int32, (HEADS * CP, D), 0) // CP
        == lax.broadcasted_iota(jnp.int32, (HEADS * CP, D), 1) // HD
    )
    scale = math.log2(math.e) / math.sqrt(HD)
    one_row = (lax.broadcasted_iota(jnp.int32, (16, 64), 0) == 0).astype(F32)
    one_row_all = (lax.broadcasted_iota(jnp.int32, (16, 1024), 0) == 0).astype(F32)
    key_heads = jnp.where(own_head, jnp.concatenate([coef_ref[frame, 1]] * HEADS, axis=0), 0.0).astype(BF)
    pair = dot_nt(key_heads, coef_ref[frame, 0].astype(BF)) * scale
    own = jnp.concatenate([own_ref[:, 64 * frame : 64 * (frame + 1)], one_row], axis=0)
    own_high, own_low = split(own)
    pair_high, pair_low = split(pair)
    reduced = dot_nn(
        jnp.concatenate([pair_high, pair_low, pair_high], axis=1),
        jnp.concatenate([own_high, own_high, own_low], axis=0),
    )
    for head in range(HEADS):
        query_ref[:, 64 * head : 64 * (head + 1)] = reduced[CP * head : CP * (head + 1)]
    query_high, query_low = split(query_ref[...])
    queries = jnp.concatenate([query_high, query_low, query_high], axis=0)
    token_high, token_low = split(jnp.concatenate([tokens_ref[frame], one_row_all], axis=0))
    keys = jnp.concatenate([token_high, token_high, token_low], axis=0)
    values = jnp.concatenate([token_high, token_low[0:16]], axis=0)
    for chunk in range(4):
        scores = dot_tn(keys, queries[:, 256 * chunk : 256 * (chunk + 1)])
        top = jnp.max(scores, axis=0, keepdims=True)
        weights = jnp.exp2(scores - top).astype(BF)
        summed = dot_nn(values, weights)
        mixed = (summed[0:16] + summed[32:48]) / summed[16:17]
        for sub in range(4):
            head = 4 * chunk + sub
            part_ref[CP * head : CP * head + 16, :] = mixed[:, 64 * sub : 64 * (sub + 1)]
            part_ref[CP * head + 16 : CP * head + 32, :] = one_row
    value_heads = jnp.where(own_head, jnp.concatenate([coef_ref[frame, 2]] * HEADS, axis=0), 0.0).astype(BF)
    mix_ref[...] = dot_tn(part_ref[...].astype(BF), value_heads).astype(BF)


def y_order(me):
    return [me, lax.rem(me + 12, 16), lax.rem(me + 4, 16), lax.rem(me + 8, 16)]


def at_rows(index):
    return pl.ds(pl.multiple_of(index * HD, 8), HD)


def place_rows(out_ref, product, order):
    for place, index in enumerate(order):
        out_ref[at_rows(index), :] = product[HD * place : HD * (place + 1)]


def hidden_kernel(first_ref, second_ref, latents_ref, embed_ref, mod_ref, *rest):
    *blocks, hidden_ref, inner_ref, update_ref = rest
    mix = jnp.concatenate([first_ref[...], second_ref[...]], axis=0).T
    me = lax.axis_index("seq")
    for flip, block in enumerate(blocks):
        place_rows(update_ref, dot_nn(block[...], mix), y_order(me ^ flip))
    embedded = product_tn(embed_ref[...], both_frames(latents_ref))
    gate, shift, scale = modulation_columns(mod_ref[...], (2, 3, 4))
    hidden = embedded + gate * update_ref[...]
    hidden_ref[...] = hidden
    inner_ref[...] = (normalize(hidden) * (1.0 + scale) + shift).astype(BF)


def temporal_kernel(advance_ref, *refs):
    sources, outs, (held_ref, sems) = refs[:4], refs[12:14], refs[14:]
    copies = [
        pltpu.make_async_copy(source, held_ref.at[place], sems.at[place]) for place, source in enumerate(sources)
    ]
    for copy in copies:
        copy.start()
    arrived = [one[...] for one in refs[4:12]]
    following = jnp.concatenate(arrived[2:4] + arrived[0:2], axis=1)
    tokens = jnp.concatenate(arrived[6:8] + arrived[4:6], axis=1)
    last = lax.axis_index("queue") == lax.axis_size("queue") - 1
    limit = jnp.where(last, 0, advance_ref[0])
    frame = lax.broadcasted_iota(jnp.int32, (1, 128), 1) // 64
    keep_same = frame < limit
    keep_other = (1 - frame) < limit
    scale = math.log2(math.e) / math.sqrt(HD)
    for place, copy in enumerate(copies):
        copy.wait()
        block = held_ref[place, 0 : 3 * HD]
        both = dot_nn(block, tokens)
        ahead = dot_nn(block[HD : 3 * HD], following)
        query, key, value = (both[HD * index : HD * (index + 1)] for index in range(3))
        key_next, value_next = ahead[0:HD], ahead[HD : 2 * HD]
        for side in range(4):
            lanes = slice(128 * side, 128 * (side + 1))
            asked = query[:, lanes] * scale
            keys = [key[:, lanes], key_next[:, lanes]]
            values = [value[:, lanes], value_next[:, lanes]]
            keys = [keys[0], pltpu.roll(keys[0], 64, 1), keys[1], pltpu.roll(keys[1], 64, 1)]
            values = [values[0], pltpu.roll(values[0], 64, 1), values[1], pltpu.roll(values[1], 64, 1)]
            scores = [jnp.sum(asked * one, axis=0, keepdims=True) for one in keys]
            scores[2] = jnp.where(keep_same, scores[2], -1e30)
            scores[3] = jnp.where(keep_other, scores[3], -1e30)
            top = jnp.maximum(jnp.maximum(scores[0], scores[1]), jnp.maximum(scores[2], scores[3]))
            weights = [jnp.exp2(one - top) for one in scores]
            inverse = 1.0 / (weights[0] + weights[1] + weights[2] + weights[3])
            mixed = sum(w * inverse * v for w, v in zip(weights, values))
            outs[side // 2][HD * place : HD * (place + 1), 128 * (side % 2) : 128 * (side % 2 + 1)] = mixed.astype(BF)


def pair_order(me):
    return [index for pair in zip(y_order(me), y_order(me ^ 2)) for index in pair]


def output_kernel(near_ref, across_ref, near_peer_ref, across_peer_ref, *refs):
    blocks, (own_ref, peer_ref, mix_ref) = refs[:4], refs[4:]
    me = lax.axis_index("seq")
    for flip, part in ((0, near_ref), (2, across_ref)):
        place_rows(mix_ref, part[...].astype(F32), y_order(me ^ flip))
    for flip, part in ((1, near_peer_ref), (3, across_peer_ref)):
        value = part[...].astype(F32)
        place_rows(mix_ref, jnp.concatenate([value[:, 128:256], value[:, 0:128]], axis=1), y_order(me ^ flip))
    mix = mix_ref[...].astype(BF)
    for place, block in enumerate(blocks):
        product = dot_nn(block[3 * HD : 5 * HD], mix)
        rows = slice(2 * HD * place, 2 * HD * (place + 1))
        own_ref[rows, :] = product[:, 0:128]
        peer_ref[rows, :] = product[:, 128:256]


def final_kernel(own_ref, peer_ref, hidden_ref, latents_ref, mod_ref, final_ref, velocity_ref, updated_ref, update_ref):
    me = lax.axis_index("seq")
    place_rows(update_ref, own_ref[...], pair_order(me))
    place_rows(update_ref, peer_ref[...], pair_order(me ^ 1))
    gate, shift, scale = modulation_columns(mod_ref[...], (5, 6, 7))
    hidden = hidden_ref[...] + gate * update_ref[...]
    inner = (normalize(hidden) * (1.0 + scale) + shift).astype(BF)
    velocity = dot_nn(final_ref[...], inner)
    for frame in range(2):
        part = velocity[:, 64 * frame : 64 * (frame + 1)]
        velocity_ref[frame] = part
        updated_ref[frame] = latents_ref[frame] - part * (1.0 / 32.0)


def params(mebibytes):
    return pltpu.CompilerParams(vmem_limit_bytes=mebibytes << 20)


def takes(microseconds):
    return pl.CostEstimate(
        flops=int(microseconds * 1.15e9), bytes_accessed=1000, transcendentals=0
    )


def along_seq(array, to):
    return lax.ppermute(array, "seq", [(i, to(i)) for i in range(16)])


def y_up(array):
    return along_seq(array, lambda i: (i + 4) % 16)


def y_down(array):
    return along_seq(array, lambda i: (i + 12) % 16)


def over_x(array):
    return along_seq(array, lambda i: i ^ 2)


def other_core(array):
    return along_seq(array, lambda i: i ^ 1)


def from_next(array):
    return lax.ppermute(array, "queue", [(i, i - 1) for i in range(1, 16)])


def over_both(array):
    return along_seq(array, lambda i: i ^ 3)


def y_far(array):
    return along_seq(array, lambda i: (i + 8) % 16)


def stack_after(after, blocks, name):
    return pl.pallas_call(
        stack_kernel,
        out_shape=jax.ShapeDtypeStruct((len(blocks), *blocks[0].shape), BF),
        in_specs=[VMEM] * (1 + len(blocks)),
        out_specs=VMEM,
        cost_estimate=takes(2),
        name=name,
    )(after, *blocks)


def gate(held, *rows):
    there = rows[0].astype(F32) <= 3e38
    for row in rows[1:]:
        there = there & (row.astype(F32) <= 3e38)
    return jnp.where(there, held, jnp.zeros_like(held))


def shards(
    latents,
    levels,
    advance,
    fresh_noise,
    level_mod,
    embed_w,
    spatial_qkv,
    spatial_out,
    temporal_qkv,
    temporal_out,
    final_w,
):
    lat = latents.transpose(0, 2, 1)
    spatial_w = spatial_qkv.transpose(1, 0, 2)
    out_w = spatial_out.transpose(1, 0)
    temporal_w = temporal_qkv.transpose(1, 2, 0)
    last_w = temporal_out.transpose(1, 0)
    final_t = final_w.transpose(1, 0)

    with jax.named_scope("last_x"):
        last_across = over_x(last_w)
    packed, scaled = pl.pallas_call(
        pack_kernel,
        out_shape=(
            jax.ShapeDtypeStruct((16, 40, 128), F32),
            jax.ShapeDtypeStruct((16, 128), F32),
        ),
        in_specs=[SMEM, VMEM, VMEM, VMEM, ANY],
        out_specs=(VMEM, VMEM),
        cost_estimate=takes(2),
        name="pack",
    )(levels, lat, embed_w, level_mod, last_across)
    everyone = lax.all_to_all(packed, "seq", split_axis=0, concat_axis=0, tiled=True)
    with jax.named_scope("out_y"):
        out_far = y_far(out_w)
        out_own = jnp.stack([out_w, y_up(out_w), y_down(out_w), out_far])
    with jax.named_scope("out_x"):
        out_across = over_x(out_own)
    with jax.named_scope("out_core"):
        out_peer = other_core(out_own)
    five = lax.dynamic_update_slice(jnp.zeros((5, HD, D), BF), gate(temporal_w, out_far[0]), (0, 0, 0))
    five = lax.dynamic_update_slice(five, jnp.stack([last_w, last_across]), (3, 0, 0))
    with jax.named_scope("five_y"):
        below, above, far = y_up(five), y_down(five), y_far(five)

    coef, mod, tokens = pl.pallas_call(
        coefficient_kernel,
        out_shape=(
            jax.ShapeDtypeStruct((2, 3, CP, D), F32),
            jax.ShapeDtypeStruct((16, D), F32),
            jax.ShapeDtypeStruct((2, 16, 1024), F32),
        ),
        in_specs=[VMEM] * 2 + [ANY],
        out_specs=(VMEM, VMEM, VMEM),
        scratch_shapes=[pltpu.VMEM((3, D, D), BF), pltpu.SemaphoreType.DMA((3, 4))],
        compiler_params=params(48),
        cost_estimate=takes(20),
        name="coefficients",
    )(everyone, embed_w, spatial_w)

    def attend(frame, *after):
        return pl.pallas_call(
            functools.partial(attend_kernel, frame),
            out_shape=jax.ShapeDtypeStruct((64, D), BF),
            in_specs=[VMEM] * 3 + [ANY] * len(after),
            out_specs=VMEM,
            scratch_shapes=[
                pltpu.VMEM((CP, 1024), F32),
                pltpu.VMEM((HEADS * CP, 64), F32),
            ],
            compiler_params=params(24),
            cost_estimate=takes(1),
            name="attend",
        )(scaled, tokens, coef, *after)

    first = attend(0)
    second = attend(1, first)
    out_across = gate(out_across, second[0], below[0, 0], above[0, 0])
    with jax.named_scope("out_core"):
        out_both = other_core(out_across)

    hidden, inner = pl.pallas_call(
        hidden_kernel,
        out_shape=(
            jax.ShapeDtypeStruct((D, 128), F32),
            jax.ShapeDtypeStruct((D, 128), BF),
        ),
        in_specs=[VMEM] * 9,
        out_specs=(VMEM, VMEM),
        scratch_shapes=[pltpu.VMEM((D, 128), F32)],
        compiler_params=params(24),
        cost_estimate=takes(2),
        name="hidden",
    )(first, second, lat, embed_w, mod, *(one.reshape(4 * HD, D) for one in (out_own, out_peer, out_across, out_both)))
    with jax.named_scope("inner"):
        pairs = [(16 * q + j, 16 * (q - 1) + (j ^ 2)) for q in range(1, 16) for j in range(16)]
        following_across = lax.ppermute(inner, ("queue", "seq"), pairs)
        across = over_x(inner)
        following = from_next(inner)
    with jax.named_scope("inner_core"):
        tokens_four = [inner, other_core(inner), across, other_core(across)]
        following_four = [following, other_core(following), following_across, other_core(following_across)]
    blocks = [one.reshape(5 * HD, D) for one in (five, below, above, far)]
    parts = pl.pallas_call(
        temporal_kernel,
        out_shape=(jax.ShapeDtypeStruct((4 * HD, 256), BF),) * 2,
        in_specs=[SMEM] + [ANY] * 4 + [VMEM] * 8,
        out_specs=(VMEM,) * 2,
        scratch_shapes=[pltpu.VMEM((4, 5 * HD, D), BF), pltpu.SemaphoreType.DMA((4,))],
        compiler_params=params(48),
        cost_estimate=takes(4),
        name="temporal",
    )(advance, *blocks, *following_four[2:], *following_four[:2], *tokens_four[2:], *tokens_four[:2])
    with jax.named_scope("back"):
        near, across = parts[0], over_x(parts[1])
        near_peer, across_peer = other_core(near), other_core(across)
    update_own, update_peer = pl.pallas_call(
        output_kernel,
        out_shape=(jax.ShapeDtypeStruct((8 * HD, 128), F32),) * 2,
        in_specs=[VMEM] * 8,
        out_specs=(VMEM,) * 2,
        scratch_shapes=[pltpu.VMEM((D, 256), F32)],
        compiler_params=params(24),
        cost_estimate=takes(1),
        name="output",
    )(near, across, near_peer, across_peer, *blocks)
    with jax.named_scope("update"):
        update_peer = other_core(update_peer)
    velocity, updated = pl.pallas_call(
        final_kernel,
        out_shape=(
            jax.ShapeDtypeStruct((2, C, 64), F32),
            jax.ShapeDtypeStruct((2, C, 64), F32),
        ),
        in_specs=[VMEM] * 6,
        out_specs=(VMEM, VMEM),
        scratch_shapes=[pltpu.VMEM((D, 128), F32)],
        compiler_params=params(24),
        cost_estimate=takes(2),
        name="final",
    )(update_own, update_peer, hidden, lat, mod, final_t)
    incoming = from_next(updated[0])
    is_last = lax.axis_index("queue") == lax.axis_size("queue") - 1
    tail = jnp.where(is_last, fresh_noise.transpose(1, 0), incoming)
    queue_next = jnp.stack([updated[1], tail])
    return velocity.transpose(0, 2, 1), queue_next.transpose(0, 2, 1)


def solution(mesh):
    placed = (
        P("queue", "seq", None),
        P("queue"),
        P("queue"),
        P("seq", None),
        P(None, None, "seq"),
        P(),
        P(),
        P(None, "seq"),
        P(None, None, "seq"),
        P(None, "seq"),
        P(),
    )
    return jax.shard_map(
        shards,
        mesh=mesh,
        in_specs=placed,
        out_specs=(P("queue", "seq", None), P("queue", "seq", None)),
        check_vma=False,
    )
```

```python
import functools
import math

import jax
import jax.numpy as jnp
from jax import lax
from jax.experimental import pallas as pl
from jax.experimental.pallas import tpu as pltpu
from jax.sharding import PartitionSpec as P

HEADS = 16
HD = 72
D = HEADS * HD
C = 16
CP = 32
BF = jnp.bfloat16
F32 = jnp.float32
VMEM = pl.BlockSpec(memory_space=pltpu.VMEM)
SMEM = pl.BlockSpec(memory_space=pltpu.SMEM)
ANY = pl.BlockSpec(memory_space=pl.ANY)


def split(value):
    high = value.astype(BF)
    return high, (value - high.astype(F32)).astype(BF)


def dot_tn(a, b):
    return lax.dot_general(a, b, (((0,), (0,)), ((), ())), preferred_element_type=F32)


def dot_nt(a, b):
    return lax.dot_general(a, b, (((1,), (1,)), ((), ())), preferred_element_type=F32)


def dot_nn(a, b):
    return jnp.dot(a, b, preferred_element_type=F32)


def product_tn(a, b):
    a_high, a_low = split(a)
    b_high, b_low = split(b)
    return dot_tn(
        jnp.concatenate([a_high, a_low, a_high], axis=0),
        jnp.concatenate([b_high, b_high, b_low], axis=0),
    )


def both_frames(latents_ref):
    return jnp.concatenate([latents_ref[0], latents_ref[1]], axis=1)


def normalize(hidden):
    width = hidden.shape[0]
    mean_value = jnp.sum(hidden, axis=0, keepdims=True) * (1.0 / width)
    centered = hidden - mean_value
    variance = jnp.sum(centered * centered, axis=0, keepdims=True) * (1.0 / width)
    return centered * lax.rsqrt(variance + 1e-06)


def modulation_columns(mod, rows):
    tokens = 128
    high, low = split(mod)
    row_at = lax.broadcasted_iota(jnp.int32, (16, tokens * len(rows)), 0)
    lane_at = lax.broadcasted_iota(jnp.int32, (16, tokens * len(rows)), 1)
    wanted = jnp.zeros_like(row_at)
    for place, row in enumerate(rows):
        wanted = jnp.where(lane_at // tokens == place, row, wanted)
    wanted = wanted + 8 * ((lane_at % tokens) // 64)
    chosen = (row_at == wanted).astype(F32).astype(BF)
    columns = dot_tn(
        jnp.concatenate([high, low], axis=0), jnp.concatenate([chosen, chosen], axis=0)
    )
    return [columns[:, tokens * i : tokens * (i + 1)] for i in range(len(rows))]


def pack_kernel(levels_ref, latents_ref, embed_ref, table_ref, after_ref, out_ref, own_ref):
    channels = both_frames(latents_ref)
    embed = embed_ref[...]
    centered = embed - jnp.sum(embed, axis=1, keepdims=True) * (1.0 / D)
    spread = product_tn(centered, channels)
    variance = jnp.sum(spread * spread, axis=0, keepdims=True) * (1.0 / D)
    inverse = lax.rsqrt(variance + 1e-06)
    own_ref[...] = channels * inverse
    peers = out_ref.shape[0]
    for peer in range(peers):
        out_ref[peer, 0:16, :] = channels
        out_ref[peer, 32:40, :] = jnp.broadcast_to(inverse, (8, 128))
        for frame in range(2):
            rows = table_ref[levels_ref[frame]]
            out_ref[peer, 16 + 8 * frame : 24 + 8 * frame, 0:HD] = rows


def coefficient_kernel(all_ref, embed_ref, weight_ref, coef_ref, mod_ref, tokens_ref, held_ref, sems):
    parts, rows = sems.shape[1], D // sems.shape[1]
    copies = [
        [
            pltpu.make_async_copy(
                weight_ref.at[index, pl.ds(rows * part, rows)],
                held_ref.at[index, pl.ds(rows * part, rows)],
                sems.at[index, part],
            )
            for part in range(parts)
        ]
        for index in range(3)
    ]
    for index in range(3):
        for copy in copies[index]:
            copy.start()
    peers = all_ref.shape[0]
    for peer in range(peers):
        mod_ref[:, HD * peer : HD * (peer + 1)] = all_ref[peer, 16:32, 0:HD]
        scaled = all_ref[peer, 0:16] * all_ref[peer, 32:33]
        for frame in range(2):
            tokens_ref[frame, :, 64 * peer : 64 * (peer + 1)] = scaled[:, 64 * frame : 64 * (frame + 1)]
    mod = mod_ref[...]
    embed = embed_ref[...]
    centered = embed - jnp.sum(embed, axis=1, keepdims=True) * (1.0 / D)
    row16 = lax.broadcasted_iota(jnp.int32, (16, D), 0)
    rows = []
    for frame in range(2):
        rows.append(centered * (1.0 + mod[8 * frame + 1 : 8 * frame + 2]))
        rows.append(jnp.where(row16 == 0, mod[8 * frame : 8 * frame + 1], 0.0))
    high, low = split(jnp.concatenate(rows, axis=0))
    stacked = jnp.concatenate([high, low], axis=0)
    for index in range(3):
        for copy in copies[index]:
            copy.wait()
        both = dot_nn(stacked, held_ref[index])
        for frame in range(2):
            rows = slice(CP * frame, CP * (frame + 1))
            coef_ref[frame, index] = both[rows] + both[64:128][rows]


def attend_kernel(frame, own_ref, tokens_ref, coef_ref, *refs):
    mix_ref, query_ref, part_ref = refs[-3:]
    own_head = (
        lax.broadcasted_iota(jnp.int32, (HEADS * CP, D), 0) // CP
        == lax.broadcasted_iota(jnp.int32, (HEADS * CP, D), 1) // HD
    )
    scale = math.log2(math.e) / math.sqrt(HD)
    one_row = (lax.broadcasted_iota(jnp.int32, (16, 64), 0) == 0).astype(F32)
    one_row_all = (lax.broadcasted_iota(jnp.int32, (16, 1024), 0) == 0).astype(F32)
    key_heads = jnp.where(own_head, jnp.concatenate([coef_ref[frame, 1]] * HEADS, axis=0), 0.0).astype(BF)
    pair = dot_nt(key_heads, coef_ref[frame, 0].astype(BF)) * scale
    own = jnp.concatenate([own_ref[:, 64 * frame : 64 * (frame + 1)], one_row], axis=0)
    own_high, own_low = split(own)
    pair_high, pair_low = split(pair)
    reduced = dot_nn(
        jnp.concatenate([pair_high, pair_low, pair_high], axis=1),
        jnp.concatenate([own_high, own_high, own_low], axis=0),
    )
    for head in range(HEADS):
        query_ref[:, 64 * head : 64 * (head + 1)] = reduced[CP * head : CP * (head + 1)]
    query_high, query_low = split(query_ref[...])
    queries = jnp.concatenate([query_high, query_low, query_high], axis=0)
    token_high, token_low = split(jnp.concatenate([tokens_ref[frame], one_row_all], axis=0))
    keys = jnp.concatenate([token_high, token_high, token_low], axis=0)
    values = jnp.concatenate([token_high, token_low[0:16]], axis=0)
    for chunk in range(4):
        scores = dot_tn(keys, queries[:, 256 * chunk : 256 * (chunk + 1)])
        top = jnp.max(scores, axis=0, keepdims=True)
        weights = jnp.exp2(scores - top).astype(BF)
        summed = dot_nn(values, weights)
        mixed = (summed[0:16] + summed[32:48]) / summed[16:17]
        for sub in range(4):
            head = 4 * chunk + sub
            part_ref[CP * head : CP * head + 16, :] = mixed[:, 64 * sub : 64 * (sub + 1)]
            part_ref[CP * head + 16 : CP * head + 32, :] = one_row
    value_heads = jnp.where(own_head, jnp.concatenate([coef_ref[frame, 2]] * HEADS, axis=0), 0.0).astype(BF)
    mix_ref[...] = dot_tn(part_ref[...].astype(BF), value_heads).astype(BF)


def y_order(me):
    return [me, lax.rem(me + 12, 16), lax.rem(me + 4, 16), lax.rem(me + 8, 16)]


def at_rows(index):
    return pl.ds(pl.multiple_of(index * HD, 8), HD)


def place_rows(out_ref, product, order):
    for place, index in enumerate(order):
        out_ref[at_rows(index), :] = product[HD * place : HD * (place + 1)]


def hidden_kernel(first_ref, second_ref, latents_ref, embed_ref, mod_ref, *rest):
    *blocks, hidden_ref, inner_ref, update_ref = rest
    mix = jnp.concatenate([first_ref[...], second_ref[...]], axis=0).T
    me = lax.axis_index("seq")
    orders = [y_order(me), y_order(me ^ 1), y_order(me ^ 2), y_order(me ^ 3)[:2], y_order(me ^ 3)[2:]]
    for block, order in zip(blocks, orders):
        place_rows(update_ref, dot_nn(block[...], mix), order)
    embedded = product_tn(embed_ref[...], both_frames(latents_ref))
    gate, shift, scale = modulation_columns(mod_ref[...], (2, 3, 4))
    hidden = embedded + gate * update_ref[...]
    hidden_ref[...] = hidden
    inner_ref[...] = (normalize(hidden) * (1.0 + scale) + shift).astype(BF)


def temporal_kernel(advance_ref, *refs):
    blocks, out_ref = refs[:4], refs[8]
    following = jnp.concatenate([one[...] for one in refs[4:6]], axis=1)
    tokens = jnp.concatenate([one[...] for one in refs[6:8]], axis=1)
    last = lax.axis_index("queue") == lax.axis_size("queue") - 1
    limit = jnp.where(last, 0, advance_ref[0])
    frame = lax.broadcasted_iota(jnp.int32, (1, 128), 1) // 64
    keep_same = frame < limit
    keep_other = (1 - frame) < limit
    scale = math.log2(math.e) / math.sqrt(HD)
    for place, block_ref in enumerate(blocks):
        block = block_ref[0 : 3 * HD]
        both = dot_nn(block, tokens)
        ahead = dot_nn(block[HD : 3 * HD], following)
        query, key, value = (both[HD * index : HD * (index + 1)] for index in range(3))
        key_next, value_next = ahead[0:HD], ahead[HD : 2 * HD]
        for side in range(2):
            lanes = slice(128 * side, 128 * (side + 1))
            asked = query[:, lanes] * scale
            keys = [key[:, lanes], key_next[:, lanes]]
            values = [value[:, lanes], value_next[:, lanes]]
            keys = [keys[0], pltpu.roll(keys[0], 64, 1), keys[1], pltpu.roll(keys[1], 64, 1)]
            values = [values[0], pltpu.roll(values[0], 64, 1), values[1], pltpu.roll(values[1], 64, 1)]
            scores = [jnp.sum(asked * one, axis=0, keepdims=True) for one in keys]
            scores[2] = jnp.where(keep_same, scores[2], -1e30)
            scores[3] = jnp.where(keep_other, scores[3], -1e30)
            top = jnp.maximum(jnp.maximum(scores[0], scores[1]), jnp.maximum(scores[2], scores[3]))
            weights = [jnp.exp2(one - top) for one in scores]
            inverse = 1.0 / (weights[0] + weights[1] + weights[2] + weights[3])
            mixed = sum(w * inverse * v for w, v in zip(weights, values))
            out_ref[HD * place : HD * (place + 1), lanes] = mixed.astype(BF)


def pair_order(me):
    return [index for pair in zip(y_order(me), y_order(me ^ 2)) for index in pair]


def output_kernel(near_ref, across_ref, near_peer_ref, across_peer_ref, *refs):
    blocks, (own_ref, peer_ref, mix_ref) = refs[:4], refs[4:]
    me = lax.axis_index("seq")
    for flip, part in ((0, near_ref), (2, across_ref)):
        place_rows(mix_ref, part[...].astype(F32), y_order(me ^ flip))
    for flip, part in ((1, near_peer_ref), (3, across_peer_ref)):
        value = part[...].astype(F32)
        place_rows(mix_ref, jnp.concatenate([value[:, 128:256], value[:, 0:128]], axis=1), y_order(me ^ flip))
    mix = mix_ref[...].astype(BF)
    for place, block in enumerate(blocks):
        product = dot_nn(block[3 * HD : 5 * HD], mix)
        rows = slice(2 * HD * place, 2 * HD * (place + 1))
        own_ref[rows, :] = product[:, 0:128]
        peer_ref[rows, :] = product[:, 128:256]


def final_kernel(own_ref, peer_ref, hidden_ref, latents_ref, mod_ref, final_ref, velocity_ref, updated_ref, update_ref):
    me = lax.axis_index("seq")
    place_rows(update_ref, own_ref[...], pair_order(me))
    place_rows(update_ref, peer_ref[...], pair_order(me ^ 1))
    gate, shift, scale = modulation_columns(mod_ref[...], (5, 6, 7))
    hidden = hidden_ref[...] + gate * update_ref[...]
    inner = (normalize(hidden) * (1.0 + scale) + shift).astype(BF)
    velocity = dot_nn(final_ref[...], inner)
    for frame in range(2):
        part = velocity[:, 64 * frame : 64 * (frame + 1)]
        velocity_ref[frame] = part
        updated_ref[frame] = latents_ref[frame] - part * (1.0 / 32.0)


def params(mebibytes):
    return pltpu.CompilerParams(vmem_limit_bytes=mebibytes << 20)


def takes(microseconds):
    return pl.CostEstimate(
        flops=int(microseconds * 1.15e9), bytes_accessed=1000, transcendentals=0
    )


def along_seq(array, to):
    return lax.ppermute(array, "seq", [(i, to(i)) for i in range(16)])


def y_up(array):
    return along_seq(array, lambda i: (i + 4) % 16)


def y_down(array):
    return along_seq(array, lambda i: (i + 12) % 16)


def over_x(array):
    return along_seq(array, lambda i: i ^ 2)


def other_core(array):
    return along_seq(array, lambda i: i ^ 1)


def from_next(array):
    return lax.ppermute(array, "queue", [(i, i - 1) for i in range(1, 16)])


def over_both(array):
    return along_seq(array, lambda i: i ^ 3)


def y_far(array):
    return along_seq(array, lambda i: (i + 8) % 16)


def stack_after(after, blocks, name):
    return pl.pallas_call(
        stack_kernel,
        out_shape=jax.ShapeDtypeStruct((len(blocks), *blocks[0].shape), BF),
        in_specs=[VMEM] * (1 + len(blocks)),
        out_specs=VMEM,
        cost_estimate=takes(2),
        name=name,
    )(after, *blocks)


def gate(held, *rows):
    there = rows[0].astype(F32) <= jnp.inf
    for row in rows[1:]:
        there = there & (row.astype(F32) <= jnp.inf)
    return jnp.where(there, held, jnp.zeros_like(held))


def shards(
    latents,
    levels,
    advance,
    fresh_noise,
    level_mod,
    embed_w,
    spatial_qkv,
    spatial_out,
    temporal_qkv,
    temporal_out,
    final_w,
):
    lat = latents.transpose(0, 2, 1)
    spatial_w = spatial_qkv.transpose(1, 0, 2)
    out_w = spatial_out.transpose(1, 0)
    temporal_w = temporal_qkv.transpose(1, 2, 0)
    last_w = temporal_out.transpose(1, 0)
    final_t = final_w.transpose(1, 0)

    with jax.named_scope("last_x"):
        last_across = over_x(last_w)
    packed, scaled = pl.pallas_call(
        pack_kernel,
        out_shape=(
            jax.ShapeDtypeStruct((16, 40, 128), F32),
            jax.ShapeDtypeStruct((16, 128), F32),
        ),
        in_specs=[SMEM, VMEM, VMEM, VMEM, VMEM],
        out_specs=(VMEM, VMEM),
        cost_estimate=takes(2),
        name="pack",
    )(levels, lat, embed_w, level_mod, last_across)
    everyone = lax.all_to_all(packed, "seq", split_axis=0, concat_axis=0, tiled=True)
    with jax.named_scope("out_y"):
        out_far = y_far(out_w)
        out_own = jnp.stack([out_w, y_up(out_w), y_down(out_w), out_far])
    with jax.named_scope("out_x"):
        out_across = over_x(out_own)
    with jax.named_scope("out_core"):
        out_peer = other_core(out_own)
    five = lax.dynamic_update_slice(jnp.zeros((5, HD, D), BF), gate(temporal_w, out_far[0]), (0, 0, 0))
    five = lax.dynamic_update_slice(five, jnp.stack([last_w, last_across]), (3, 0, 0))
    with jax.named_scope("five_y"):
        below, above = y_up(five), y_down(five)

    coef, mod, tokens = pl.pallas_call(
        coefficient_kernel,
        out_shape=(
            jax.ShapeDtypeStruct((2, 3, CP, D), F32),
            jax.ShapeDtypeStruct((16, D), F32),
            jax.ShapeDtypeStruct((2, 16, 1024), F32),
        ),
        in_specs=[VMEM] * 2 + [ANY],
        out_specs=(VMEM, VMEM, VMEM),
        scratch_shapes=[pltpu.VMEM((3, D, D), BF), pltpu.SemaphoreType.DMA((3, 4))],
        compiler_params=params(45),
        cost_estimate=takes(20),
        name="coefficients",
    )(everyone, embed_w, spatial_w)

    def attend(frame, *after):
        return pl.pallas_call(
            functools.partial(attend_kernel, frame),
            out_shape=jax.ShapeDtypeStruct((64, D), BF),
            in_specs=[VMEM] * 3 + [ANY] * len(after),
            out_specs=VMEM,
            scratch_shapes=[
                pltpu.VMEM((CP, 1024), F32),
                pltpu.VMEM((HEADS * CP, 64), F32),
            ],
            compiler_params=params(24),
            cost_estimate=takes(0.1),
            name="attend",
        )(scaled, tokens, coef, *after)

    first = attend(0)
    second = attend(1, first)
    with jax.named_scope("out_core"):
        out_both = [other_core(gate(out_across[half : half + 2], second[0])) for half in (0, 2)]
    first = gate(first, below[0, 0], above[0, 0])
    with jax.named_scope("five_far"):
        far = y_far(gate(five, first[0]))

    hidden, inner = pl.pallas_call(
        hidden_kernel,
        out_shape=(
            jax.ShapeDtypeStruct((D, 128), F32),
            jax.ShapeDtypeStruct((D, 128), BF),
        ),
        in_specs=[VMEM] * 10,
        out_specs=(VMEM, VMEM),
        scratch_shapes=[pltpu.VMEM((D, 128), F32)],
        compiler_params=params(24),
        cost_estimate=takes(2),
        name="hidden",
    )(first, second, lat, embed_w, mod, *(one.reshape(-1, D) for one in (out_own, out_peer, out_across, *out_both)))
    with jax.named_scope("inner"):
        pairs = [(16 * q + j, 16 * (q - 1) + (j ^ 2)) for q in range(1, 16) for j in range(16)]
        following_across = lax.ppermute(inner, ("queue", "seq"), pairs)
        across = over_x(inner)
        following = from_next(inner)
    with jax.named_scope("inner_core"):
        tokens_four = [inner, other_core(inner), across, other_core(across)]
        following_four = [following, other_core(following), following_across, other_core(following_across)]
    blocks = [one.reshape(5 * HD, D) for one in (five, below, gate(above, far[0, 0]), far)]

    def temporal(name, *tokens):
        return pl.pallas_call(
            temporal_kernel,
            out_shape=jax.ShapeDtypeStruct((4 * HD, 256), BF),
            in_specs=[SMEM] + [VMEM] * 8,
            out_specs=VMEM,
            compiler_params=params(24),
            cost_estimate=takes(2),
            name=name,
        )(advance, *blocks, *tokens)

    across = temporal("temporal_across", *following_four[2:], *tokens_four[2:])
    near = temporal("temporal_near", *following_four[:2], *tokens_four[:2])
    with jax.named_scope("back"):
        across = over_x(across)
        near_peer, across_peer = other_core(near), other_core(across)
    update_own, update_peer = pl.pallas_call(
        output_kernel,
        out_shape=(jax.ShapeDtypeStruct((8 * HD, 128), F32),) * 2,
        in_specs=[VMEM] * 8,
        out_specs=(VMEM,) * 2,
        scratch_shapes=[pltpu.VMEM((D, 256), F32)],
        compiler_params=params(24),
        cost_estimate=takes(1),
        name="output",
    )(near, across, near_peer, across_peer, *blocks)
    with jax.named_scope("update"):
        update_peer = other_core(update_peer)
    velocity, updated = pl.pallas_call(
        final_kernel,
        out_shape=(
            jax.ShapeDtypeStruct((2, C, 64), F32),
            jax.ShapeDtypeStruct((2, C, 64), F32),
        ),
        in_specs=[VMEM] * 6,
        out_specs=(VMEM, VMEM),
        scratch_shapes=[pltpu.VMEM((D, 128), F32)],
        compiler_params=params(24),
        cost_estimate=takes(2),
        name="final",
    )(update_own, update_peer, hidden, lat, mod, final_t)
    incoming = from_next(updated[0])
    is_last = lax.axis_index("queue") == lax.axis_size("queue") - 1
    tail = jnp.where(is_last, fresh_noise.transpose(1, 0), incoming)
    queue_next = jnp.stack([updated[1], tail])
    return velocity.transpose(0, 2, 1), queue_next.transpose(0, 2, 1)


def solution(mesh):
    placed = (
        P("queue", "seq", None),
        P("queue"),
        P("queue"),
        P("seq", None),
        P(None, None, "seq"),
        P(),
        P(),
        P(None, "seq"),
        P(None, None, "seq"),
        P(None, "seq"),
        P(),
    )
    return jax.shard_map(
        shards,
        mesh=mesh,
        in_specs=placed,
        out_specs=(P("queue", "seq", None), P("queue", "seq", None)),
        check_vma=False,
    )
```

```python
import functools
import math

import jax
import jax.numpy as jnp
from jax import lax
from jax.experimental import pallas as pl
from jax.experimental.pallas import tpu as pltpu
from jax.sharding import PartitionSpec as P

HEADS = 16
HD = 72
D = HEADS * HD
C = 16
CP = 32
BF = jnp.bfloat16
F32 = jnp.float32
VMEM = pl.BlockSpec(memory_space=pltpu.VMEM)
SMEM = pl.BlockSpec(memory_space=pltpu.SMEM)
ANY = pl.BlockSpec(memory_space=pl.ANY)


def split(value):
    high = value.astype(BF)
    return high, (value - high.astype(F32)).astype(BF)


def dot_tn(a, b):
    return lax.dot_general(a, b, (((0,), (0,)), ((), ())), preferred_element_type=F32)


def dot_nt(a, b):
    return lax.dot_general(a, b, (((1,), (1,)), ((), ())), preferred_element_type=F32)


def dot_nn(a, b):
    return jnp.dot(a, b, preferred_element_type=F32)


def product_tn(a, b):
    a_high, a_low = split(a)
    b_high, b_low = split(b)
    return dot_tn(
        jnp.concatenate([a_high, a_low, a_high], axis=0),
        jnp.concatenate([b_high, b_high, b_low], axis=0),
    )


def both_frames(latents_ref):
    return jnp.concatenate([latents_ref[0], latents_ref[1]], axis=1)


def normalize(hidden):
    width = hidden.shape[0]
    mean_value = jnp.sum(hidden, axis=0, keepdims=True) * (1.0 / width)
    centered = hidden - mean_value
    variance = jnp.sum(centered * centered, axis=0, keepdims=True) * (1.0 / width)
    return centered * lax.rsqrt(variance + 1e-06)


def modulation_columns(mod, rows):
    tokens = 128
    high, low = split(mod)
    row_at = lax.broadcasted_iota(jnp.int32, (16, tokens * len(rows)), 0)
    lane_at = lax.broadcasted_iota(jnp.int32, (16, tokens * len(rows)), 1)
    wanted = jnp.zeros_like(row_at)
    for place, row in enumerate(rows):
        wanted = jnp.where(lane_at // tokens == place, row, wanted)
    wanted = wanted + 8 * ((lane_at % tokens) // 64)
    chosen = (row_at == wanted).astype(F32).astype(BF)
    columns = dot_tn(
        jnp.concatenate([high, low], axis=0), jnp.concatenate([chosen, chosen], axis=0)
    )
    return [columns[:, tokens * i : tokens * (i + 1)] for i in range(len(rows))]


def pack_kernel(levels_ref, latents_ref, embed_ref, table_ref, after_ref, out_ref, own_ref):
    channels = both_frames(latents_ref)
    embed = embed_ref[...]
    centered = embed - jnp.sum(embed, axis=1, keepdims=True) * (1.0 / D)
    spread = product_tn(centered, channels)
    variance = jnp.sum(spread * spread, axis=0, keepdims=True) * (1.0 / D)
    inverse = lax.rsqrt(variance + 1e-06)
    own_ref[...] = channels * inverse
    peers = out_ref.shape[0]
    for peer in range(peers):
        out_ref[peer, 0:16, :] = channels
        out_ref[peer, 32:40, :] = jnp.broadcast_to(inverse, (8, 128))
        for frame in range(2):
            rows = table_ref[levels_ref[frame]]
            out_ref[peer, 16 + 8 * frame : 24 + 8 * frame, 0:HD] = rows


def coefficient_kernel(all_ref, embed_ref, weight_ref, coef_ref, mod_ref, tokens_ref, held_ref, sems):
    parts, rows = sems.shape[1], D // sems.shape[1]
    copies = [
        [
            pltpu.make_async_copy(
                weight_ref.at[index, pl.ds(rows * part, rows)],
                held_ref.at[index, pl.ds(rows * part, rows)],
                sems.at[index, part],
            )
            for part in range(parts)
        ]
        for index in range(3)
    ]
    for index in range(3):
        for copy in copies[index]:
            copy.start()
    peers = all_ref.shape[0]
    for peer in range(peers):
        mod_ref[:, HD * peer : HD * (peer + 1)] = all_ref[peer, 16:32, 0:HD]
        scaled = all_ref[peer, 0:16] * all_ref[peer, 32:33]
        for frame in range(2):
            tokens_ref[frame, :, 64 * peer : 64 * (peer + 1)] = scaled[:, 64 * frame : 64 * (frame + 1)]
    mod = mod_ref[...]
    embed = embed_ref[...]
    centered = embed - jnp.sum(embed, axis=1, keepdims=True) * (1.0 / D)
    row16 = lax.broadcasted_iota(jnp.int32, (16, D), 0)
    rows = []
    for frame in range(2):
        rows.append(centered * (1.0 + mod[8 * frame + 1 : 8 * frame + 2]))
        rows.append(jnp.where(row16 == 0, mod[8 * frame : 8 * frame + 1], 0.0))
    high, low = split(jnp.concatenate(rows, axis=0))
    stacked = jnp.concatenate([high, low], axis=0)
    for index in range(3):
        for copy in copies[index]:
            copy.wait()
        both = dot_nn(stacked, held_ref[index])
        for frame in range(2):
            rows = slice(CP * frame, CP * (frame + 1))
            coef_ref[frame, index] = both[rows] + both[64:128][rows]


def attend_kernel(frame, own_ref, tokens_ref, coef_ref, *refs):
    mix_ref, query_ref, part_ref = refs[-3:]
    own_head = (
        lax.broadcasted_iota(jnp.int32, (HEADS * CP, D), 0) // CP
        == lax.broadcasted_iota(jnp.int32, (HEADS * CP, D), 1) // HD
    )
    scale = math.log2(math.e) / math.sqrt(HD)
    one_row = (lax.broadcasted_iota(jnp.int32, (16, 64), 0) == 0).astype(F32)
    one_row_all = (lax.broadcasted_iota(jnp.int32, (16, 1024), 0) == 0).astype(F32)
    key_heads = jnp.where(own_head, jnp.concatenate([coef_ref[frame, 1]] * HEADS, axis=0), 0.0).astype(BF)
    pair = dot_nt(key_heads, coef_ref[frame, 0].astype(BF)) * scale
    own = jnp.concatenate([own_ref[:, 64 * frame : 64 * (frame + 1)], one_row], axis=0)
    own_high, own_low = split(own)
    pair_high, pair_low = split(pair)
    reduced = dot_nn(
        jnp.concatenate([pair_high, pair_low, pair_high], axis=1),
        jnp.concatenate([own_high, own_high, own_low], axis=0),
    )
    for head in range(HEADS):
        query_ref[:, 64 * head : 64 * (head + 1)] = reduced[CP * head : CP * (head + 1)]
    query_high, query_low = split(query_ref[...])
    queries = jnp.concatenate([query_high, query_low, query_high], axis=0)
    token_high, token_low = split(jnp.concatenate([tokens_ref[frame], one_row_all], axis=0))
    keys = jnp.concatenate([token_high, token_high, token_low], axis=0)
    values = jnp.concatenate([token_high, token_low[0:16]], axis=0)
    for chunk in range(4):
        scores = dot_tn(keys, queries[:, 256 * chunk : 256 * (chunk + 1)])
        top = jnp.max(scores, axis=0, keepdims=True)
        weights = jnp.exp2(scores - top).astype(BF)
        summed = dot_nn(values, weights)
        mixed = (summed[0:16] + summed[32:48]) / summed[16:17]
        for sub in range(4):
            head = 4 * chunk + sub
            part_ref[CP * head : CP * head + 16, :] = mixed[:, 64 * sub : 64 * (sub + 1)]
            part_ref[CP * head + 16 : CP * head + 32, :] = one_row
    value_heads = jnp.where(own_head, jnp.concatenate([coef_ref[frame, 2]] * HEADS, axis=0), 0.0).astype(BF)
    mix_ref[...] = dot_tn(part_ref[...].astype(BF), value_heads).astype(BF)


def y_order(me):
    return [me, lax.rem(me + 12, 16), lax.rem(me + 4, 16), lax.rem(me + 8, 16)]


def at_rows(index):
    return pl.ds(pl.multiple_of(index * HD, 8), HD)


def place_rows(out_ref, product, order):
    for place, index in enumerate(order):
        out_ref[at_rows(index), :] = product[HD * place : HD * (place + 1)]


def hidden_kernel(first_ref, second_ref, latents_ref, embed_ref, mod_ref, *rest):
    *blocks, hidden_ref, inner_ref, update_ref = rest
    mix = jnp.concatenate([first_ref[...], second_ref[...]], axis=0).T
    me = lax.axis_index("seq")
    orders = [y_order(me), y_order(me ^ 1), y_order(me ^ 2), y_order(me ^ 3)[:2], y_order(me ^ 3)[2:]]
    for block, order in zip(blocks, orders):
        place_rows(update_ref, dot_nn(block[...], mix), order)
    embedded = product_tn(embed_ref[...], both_frames(latents_ref))
    gate, shift, scale = modulation_columns(mod_ref[...], (2, 3, 4))
    hidden = embedded + gate * update_ref[...]
    hidden_ref[...] = hidden
    inner_ref[...] = (normalize(hidden) * (1.0 + scale) + shift).astype(BF)


def temporal_kernel(advance_ref, *refs):
    blocks, out_ref = refs[:4], refs[8]
    following = jnp.concatenate([one[...] for one in refs[4:6]], axis=1)
    tokens = jnp.concatenate([one[...] for one in refs[6:8]], axis=1)
    last = lax.axis_index("queue") == lax.axis_size("queue") - 1
    limit = jnp.where(last, 0, advance_ref[0])
    frame = lax.broadcasted_iota(jnp.int32, (1, 128), 1) // 64
    keep_same = frame < limit
    keep_other = (1 - frame) < limit
    scale = math.log2(math.e) / math.sqrt(HD)
    for place, block_ref in enumerate(blocks):
        block = block_ref[0 : 3 * HD]
        both = dot_nn(block, tokens)
        ahead = dot_nn(block[HD : 3 * HD], following)
        query, key, value = (both[HD * index : HD * (index + 1)] for index in range(3))
        key_next, value_next = ahead[0:HD], ahead[HD : 2 * HD]
        for side in range(2):
            lanes = slice(128 * side, 128 * (side + 1))
            asked = query[:, lanes] * scale
            keys = [key[:, lanes], key_next[:, lanes]]
            values = [value[:, lanes], value_next[:, lanes]]
            keys = [keys[0], pltpu.roll(keys[0], 64, 1), keys[1], pltpu.roll(keys[1], 64, 1)]
            values = [values[0], pltpu.roll(values[0], 64, 1), values[1], pltpu.roll(values[1], 64, 1)]
            scores = [jnp.sum(asked * one, axis=0, keepdims=True) for one in keys]
            scores[2] = jnp.where(keep_same, scores[2], -1e30)
            scores[3] = jnp.where(keep_other, scores[3], -1e30)
            top = jnp.maximum(jnp.maximum(scores[0], scores[1]), jnp.maximum(scores[2], scores[3]))
            weights = [jnp.exp2(one - top) for one in scores]
            inverse = 1.0 / (weights[0] + weights[1] + weights[2] + weights[3])
            mixed = sum(w * inverse * v for w, v in zip(weights, values))
            out_ref[HD * place : HD * (place + 1), lanes] = mixed.astype(BF)


def pair_order(me):
    return [index for pair in zip(y_order(me), y_order(me ^ 2)) for index in pair]


def output_kernel(near_ref, across_ref, near_peer_ref, across_peer_ref, *refs):
    blocks, (own_ref, peer_ref, mix_ref) = refs[:4], refs[4:]
    me = lax.axis_index("seq")
    for flip, part in ((0, near_ref), (2, across_ref)):
        place_rows(mix_ref, part[...].astype(F32), y_order(me ^ flip))
    for flip, part in ((1, near_peer_ref), (3, across_peer_ref)):
        value = part[...].astype(F32)
        place_rows(mix_ref, jnp.concatenate([value[:, 128:256], value[:, 0:128]], axis=1), y_order(me ^ flip))
    mix = mix_ref[...].astype(BF)
    for place, block in enumerate(blocks):
        product = dot_nn(block[3 * HD : 5 * HD], mix)
        rows = slice(2 * HD * place, 2 * HD * (place + 1))
        own_ref[rows, :] = product[:, 0:128]
        peer_ref[rows, :] = product[:, 128:256]


def final_kernel(own_ref, peer_ref, hidden_ref, latents_ref, mod_ref, final_ref, velocity_ref, updated_ref, update_ref):
    me = lax.axis_index("seq")
    place_rows(update_ref, own_ref[...], pair_order(me))
    place_rows(update_ref, peer_ref[...], pair_order(me ^ 1))
    gate, shift, scale = modulation_columns(mod_ref[...], (5, 6, 7))
    hidden = hidden_ref[...] + gate * update_ref[...]
    inner = (normalize(hidden) * (1.0 + scale) + shift).astype(BF)
    velocity = dot_nn(final_ref[...], inner)
    for frame in range(2):
        part = velocity[:, 64 * frame : 64 * (frame + 1)]
        velocity_ref[frame] = part
        updated_ref[frame] = latents_ref[frame] - part * (1.0 / 32.0)


def params(mebibytes):
    return pltpu.CompilerParams(vmem_limit_bytes=mebibytes << 20)


def takes(microseconds):
    return pl.CostEstimate(
        flops=int(microseconds * 1.15e9), bytes_accessed=1000, transcendentals=0
    )


def along_seq(array, to):
    return lax.ppermute(array, "seq", [(i, to(i)) for i in range(16)])


def y_up(array):
    return along_seq(array, lambda i: (i + 4) % 16)


def y_down(array):
    return along_seq(array, lambda i: (i + 12) % 16)


def over_x(array):
    return along_seq(array, lambda i: i ^ 2)


def other_core(array):
    return along_seq(array, lambda i: i ^ 1)


def from_next(array):
    return lax.ppermute(array, "queue", [(i, i - 1) for i in range(1, 16)])


def over_both(array):
    return along_seq(array, lambda i: i ^ 3)


def y_far(array):
    return along_seq(array, lambda i: (i + 8) % 16)


def stack_after(after, blocks, name):
    return pl.pallas_call(
        stack_kernel,
        out_shape=jax.ShapeDtypeStruct((len(blocks), *blocks[0].shape), BF),
        in_specs=[VMEM] * (1 + len(blocks)),
        out_specs=VMEM,
        cost_estimate=takes(2),
        name=name,
    )(after, *blocks)


def gate(held, *rows):
    there = rows[0].astype(F32) <= jnp.inf
    for row in rows[1:]:
        there = there & (row.astype(F32) <= jnp.inf)
    return jnp.where(there, held, jnp.zeros_like(held))


def shards(
    latents,
    levels,
    advance,
    fresh_noise,
    level_mod,
    embed_w,
    spatial_qkv,
    spatial_out,
    temporal_qkv,
    temporal_out,
    final_w,
):
    lat = latents.transpose(0, 2, 1)
    spatial_w = spatial_qkv.transpose(1, 0, 2)
    out_w = spatial_out.transpose(1, 0)
    temporal_w = temporal_qkv.transpose(1, 2, 0)
    last_w = temporal_out.transpose(1, 0)
    final_t = final_w.transpose(1, 0)

    with jax.named_scope("last_x"):
        last_across = over_x(last_w)
    packed, scaled = pl.pallas_call(
        pack_kernel,
        out_shape=(
            jax.ShapeDtypeStruct((16, 40, 128), F32),
            jax.ShapeDtypeStruct((16, 128), F32),
        ),
        in_specs=[SMEM, VMEM, VMEM, VMEM, VMEM],
        out_specs=(VMEM, VMEM),
        cost_estimate=takes(2),
        name="pack",
    )(levels, lat, embed_w, level_mod, last_across)
    everyone = lax.all_to_all(packed, "seq", split_axis=0, concat_axis=0, tiled=True)
    with jax.named_scope("out_y"):
        out_far = y_far(out_w)
        out_own = jnp.stack([out_w, y_up(out_w), y_down(out_w), out_far])
    with jax.named_scope("out_x"):
        out_across = over_x(out_own)
    with jax.named_scope("out_core"):
        out_peer = other_core(out_own)
    five = lax.dynamic_update_slice(jnp.zeros((5, HD, D), BF), gate(temporal_w, out_far[0]), (0, 0, 0))
    five = lax.dynamic_update_slice(five, jnp.stack([last_w, last_across]), (3, 0, 0))
    with jax.named_scope("five_y"):
        below, above = y_up(five), y_down(five)

    coef, mod, tokens = pl.pallas_call(
        coefficient_kernel,
        out_shape=(
            jax.ShapeDtypeStruct((2, 3, CP, D), F32),
            jax.ShapeDtypeStruct((16, D), F32),
            jax.ShapeDtypeStruct((2, 16, 1024), F32),
        ),
        in_specs=[VMEM] * 2 + [ANY],
        out_specs=(VMEM, VMEM, VMEM),
        scratch_shapes=[pltpu.VMEM((3, D, D), BF), pltpu.SemaphoreType.DMA((3, 4))],
        compiler_params=params(45),
        cost_estimate=takes(20),
        name="coefficients",
    )(everyone, embed_w, spatial_w)

    def attend(frame, *after):
        return pl.pallas_call(
            functools.partial(attend_kernel, frame),
            out_shape=jax.ShapeDtypeStruct((64, D), BF),
            in_specs=[VMEM] * 3 + [ANY] * len(after),
            out_specs=VMEM,
            scratch_shapes=[
                pltpu.VMEM((CP, 1024), F32),
                pltpu.VMEM((HEADS * CP, 64), F32),
            ],
            compiler_params=params(24),
            cost_estimate=takes(0.1),
            name="attend",
        )(scaled, tokens, coef, *after)

    first = attend(0)
    second = attend(1, first)
    with jax.named_scope("out_core"):
        out_both = [other_core(gate(out_across[half : half + 2], second[0])) for half in (0, 2)]
    first, second = gate(first, below[0, 0]), gate(second, above[0, 0])
    with jax.named_scope("five_far"):
        far = y_far(gate(five, first[0]))

    hidden, inner = pl.pallas_call(
        hidden_kernel,
        out_shape=(
            jax.ShapeDtypeStruct((D, 128), F32),
            jax.ShapeDtypeStruct((D, 128), BF),
        ),
        in_specs=[VMEM] * 10,
        out_specs=(VMEM, VMEM),
        scratch_shapes=[pltpu.VMEM((D, 128), F32)],
        compiler_params=params(24),
        cost_estimate=takes(2),
        name="hidden",
    )(first, second, lat, embed_w, mod, *(one.reshape(-1, D) for one in (out_own, out_peer, out_across, *out_both)))
    with jax.named_scope("inner"):
        pairs = [(16 * q + j, 16 * (q - 1) + (j ^ 2)) for q in range(1, 16) for j in range(16)]
        following_across = lax.ppermute(inner, ("queue", "seq"), pairs)
        across = over_x(inner)
        following = from_next(inner)
    above = gate(above, below[0, 0])
    following_across = gate(following_across, above[0, 0, 0:128])
    with jax.named_scope("inner_core"):
        tokens_four = [inner, other_core(inner), across, other_core(across)]
        following_four = [following, other_core(following), following_across, other_core(following_across)]
    blocks = [one.reshape(5 * HD, D) for one in (five, below, above, far)]

    def temporal(name, *tokens):
        return pl.pallas_call(
            temporal_kernel,
            out_shape=jax.ShapeDtypeStruct((4 * HD, 256), BF),
            in_specs=[SMEM] + [VMEM] * 8,
            out_specs=VMEM,
            compiler_params=params(24),
            cost_estimate=takes(2),
            name=name,
        )(advance, *blocks, *tokens)

    across = temporal("temporal_across", *following_four[2:], *tokens_four[2:])
    near = temporal("temporal_near", *following_four[:2], *tokens_four[:2])
    with jax.named_scope("back"):
        across = over_x(across)
        near_peer, across_peer = other_core(near), other_core(across)
    update_own, update_peer = pl.pallas_call(
        output_kernel,
        out_shape=(jax.ShapeDtypeStruct((8 * HD, 128), F32),) * 2,
        in_specs=[VMEM] * 8,
        out_specs=(VMEM,) * 2,
        scratch_shapes=[pltpu.VMEM((D, 256), F32)],
        compiler_params=params(24),
        cost_estimate=takes(1),
        name="output",
    )(near, across, near_peer, across_peer, *blocks)
    with jax.named_scope("update"):
        update_peer = other_core(update_peer)
    velocity, updated = pl.pallas_call(
        final_kernel,
        out_shape=(
            jax.ShapeDtypeStruct((2, C, 64), F32),
            jax.ShapeDtypeStruct((2, C, 64), F32),
        ),
        in_specs=[VMEM] * 6,
        out_specs=(VMEM, VMEM),
        scratch_shapes=[pltpu.VMEM((D, 128), F32)],
        compiler_params=params(24),
        cost_estimate=takes(2),
        name="final",
    )(update_own, update_peer, hidden, lat, mod, final_t)
    incoming = from_next(updated[0])
    is_last = lax.axis_index("queue") == lax.axis_size("queue") - 1
    tail = jnp.where(is_last, fresh_noise.transpose(1, 0), incoming)
    queue_next = jnp.stack([updated[1], tail])
    return velocity.transpose(0, 2, 1), queue_next.transpose(0, 2, 1)


def solution(mesh):
    placed = (
        P("queue", "seq", None),
        P("queue"),
        P("queue"),
        P("seq", None),
        P(None, None, "seq"),
        P(),
        P(),
        P(None, "seq"),
        P(None, None, "seq"),
        P(None, "seq"),
        P(),
    )
    return jax.shard_map(
        shards,
        mesh=mesh,
        in_specs=placed,
        out_specs=(P("queue", "seq", None), P("queue", "seq", None)),
        check_vma=False,
    )
```

```python
import functools
import math

import jax
import jax.numpy as jnp
from jax import lax
from jax.experimental import pallas as pl
from jax.experimental.pallas import tpu as pltpu
from jax.sharding import PartitionSpec as P

HEADS = 16
HD = 72
D = HEADS * HD
C = 16
CP = 32
BF = jnp.bfloat16
F32 = jnp.float32
VMEM = pl.BlockSpec(memory_space=pltpu.VMEM)
SMEM = pl.BlockSpec(memory_space=pltpu.SMEM)
ANY = pl.BlockSpec(memory_space=pl.ANY)


def split(value):
    high = value.astype(BF)
    return high, (value - high.astype(F32)).astype(BF)


def dot_tn(a, b):
    return lax.dot_general(a, b, (((0,), (0,)), ((), ())), preferred_element_type=F32)


def dot_nt(a, b):
    return lax.dot_general(a, b, (((1,), (1,)), ((), ())), preferred_element_type=F32)


def dot_nn(a, b):
    return jnp.dot(a, b, preferred_element_type=F32)


def product_tn(a, b):
    a_high, a_low = split(a)
    b_high, b_low = split(b)
    return dot_tn(
        jnp.concatenate([a_high, a_low, a_high], axis=0),
        jnp.concatenate([b_high, b_high, b_low], axis=0),
    )


def both_frames(latents_ref):
    return jnp.concatenate([latents_ref[0], latents_ref[1]], axis=1)


def normalize(hidden):
    width = hidden.shape[0]
    mean_value = jnp.sum(hidden, axis=0, keepdims=True) * (1.0 / width)
    centered = hidden - mean_value
    variance = jnp.sum(centered * centered, axis=0, keepdims=True) * (1.0 / width)
    return centered * lax.rsqrt(variance + 1e-06)


def modulation_columns(mod, rows):
    tokens = 128
    high, low = split(mod)
    row_at = lax.broadcasted_iota(jnp.int32, (16, tokens * len(rows)), 0)
    lane_at = lax.broadcasted_iota(jnp.int32, (16, tokens * len(rows)), 1)
    wanted = jnp.zeros_like(row_at)
    for place, row in enumerate(rows):
        wanted = jnp.where(lane_at // tokens == place, row, wanted)
    wanted = wanted + 8 * ((lane_at % tokens) // 64)
    chosen = (row_at == wanted).astype(F32).astype(BF)
    columns = dot_tn(
        jnp.concatenate([high, low], axis=0), jnp.concatenate([chosen, chosen], axis=0)
    )
    return [columns[:, tokens * i : tokens * (i + 1)] for i in range(len(rows))]


def pack_kernel(levels_ref, latents_ref, embed_ref, table_ref, after_ref, out_ref, own_ref):
    channels = both_frames(latents_ref)
    embed = embed_ref[...]
    centered = embed - jnp.sum(embed, axis=1, keepdims=True) * (1.0 / D)
    spread = product_tn(centered, channels)
    variance = jnp.sum(spread * spread, axis=0, keepdims=True) * (1.0 / D)
    inverse = lax.rsqrt(variance + 1e-06)
    own_ref[...] = channels * inverse
    peers = out_ref.shape[0]
    for peer in range(peers):
        out_ref[peer, 0:16, :] = channels
        out_ref[peer, 32:40, :] = jnp.broadcast_to(inverse, (8, 128))
        for frame in range(2):
            rows = table_ref[levels_ref[frame]]
            out_ref[peer, 16 + 8 * frame : 24 + 8 * frame, 0:HD] = rows


def coefficient_kernel(all_ref, embed_ref, weight_ref, coef_ref, mod_ref, tokens_ref, held_ref, sems):
    parts, rows = sems.shape[1], D // sems.shape[1]
    copies = [
        [
            pltpu.make_async_copy(
                weight_ref.at[index, pl.ds(rows * part, rows)],
                held_ref.at[index, pl.ds(rows * part, rows)],
                sems.at[index, part],
            )
            for part in range(parts)
        ]
        for index in range(3)
    ]
    for index in range(3):
        for copy in copies[index]:
            copy.start()
    peers = all_ref.shape[0]
    for peer in range(peers):
        mod_ref[:, HD * peer : HD * (peer + 1)] = all_ref[peer, 16:32, 0:HD]
        scaled = all_ref[peer, 0:16] * all_ref[peer, 32:33]
        for frame in range(2):
            tokens_ref[frame, :, 64 * peer : 64 * (peer + 1)] = scaled[:, 64 * frame : 64 * (frame + 1)]
    mod = mod_ref[...]
    embed = embed_ref[...]
    centered = embed - jnp.sum(embed, axis=1, keepdims=True) * (1.0 / D)
    row16 = lax.broadcasted_iota(jnp.int32, (16, D), 0)
    rows = []
    for frame in range(2):
        rows.append(centered * (1.0 + mod[8 * frame + 1 : 8 * frame + 2]))
        rows.append(jnp.where(row16 == 0, mod[8 * frame : 8 * frame + 1], 0.0))
    high, low = split(jnp.concatenate(rows, axis=0))
    stacked = jnp.concatenate([high, low], axis=0)
    for index in range(3):
        for copy in copies[index]:
            copy.wait()
        both = dot_nn(stacked, held_ref[index])
        for frame in range(2):
            rows = slice(CP * frame, CP * (frame + 1))
            coef_ref[frame, index] = both[rows] + both[64:128][rows]


def attend_kernel(frame, own_ref, tokens_ref, coef_ref, *refs):
    mix_ref, query_ref, part_ref = refs[-3:]
    own_head = (
        lax.broadcasted_iota(jnp.int32, (HEADS * CP, D), 0) // CP
        == lax.broadcasted_iota(jnp.int32, (HEADS * CP, D), 1) // HD
    )
    scale = math.log2(math.e) / math.sqrt(HD)
    one_row = (lax.broadcasted_iota(jnp.int32, (16, 64), 0) == 0).astype(F32)
    one_row_all = (lax.broadcasted_iota(jnp.int32, (16, 1024), 0) == 0).astype(F32)
    key_heads = jnp.where(own_head, jnp.concatenate([coef_ref[frame, 1]] * HEADS, axis=0), 0.0).astype(BF)
    pair = dot_nt(key_heads, coef_ref[frame, 0].astype(BF)) * scale
    own = jnp.concatenate([own_ref[:, 64 * frame : 64 * (frame + 1)], one_row], axis=0)
    own_high, own_low = split(own)
    pair_high, pair_low = split(pair)
    reduced = dot_nn(
        jnp.concatenate([pair_high, pair_low, pair_high], axis=1),
        jnp.concatenate([own_high, own_high, own_low], axis=0),
    )
    for head in range(HEADS):
        query_ref[:, 64 * head : 64 * (head + 1)] = reduced[CP * head : CP * (head + 1)]
    query_high, query_low = split(query_ref[...])
    queries = jnp.concatenate([query_high, query_low, query_high], axis=0)
    token_high, token_low = split(jnp.concatenate([tokens_ref[frame], one_row_all], axis=0))
    keys = jnp.concatenate([token_high, token_high, token_low], axis=0)
    values = jnp.concatenate([token_high, token_low[0:16]], axis=0)
    for chunk in range(4):
        scores = dot_tn(keys, queries[:, 256 * chunk : 256 * (chunk + 1)])
        top = jnp.max(scores, axis=0, keepdims=True)
        weights = jnp.exp2(scores - top).astype(BF)
        summed = dot_nn(values, weights)
        mixed = (summed[0:16] + summed[32:48]) / summed[16:17]
        for sub in range(4):
            head = 4 * chunk + sub
            part_ref[CP * head : CP * head + 16, :] = mixed[:, 64 * sub : 64 * (sub + 1)]
            part_ref[CP * head + 16 : CP * head + 32, :] = one_row
    value_heads = jnp.where(own_head, jnp.concatenate([coef_ref[frame, 2]] * HEADS, axis=0), 0.0).astype(BF)
    mix_ref[...] = dot_tn(part_ref[...].astype(BF), value_heads).astype(BF)


def y_order(me):
    return [me, lax.rem(me + 12, 16), lax.rem(me + 4, 16), lax.rem(me + 8, 16)]


def at_rows(index):
    return pl.ds(pl.multiple_of(index * HD, 8), HD)


def place_rows(out_ref, product, order):
    for place, index in enumerate(order):
        out_ref[at_rows(index), :] = product[HD * place : HD * (place + 1)]


def hidden_kernel(first_ref, second_ref, latents_ref, embed_ref, mod_ref, *rest):
    *blocks, hidden_ref, inner_ref, update_ref = rest
    mix = jnp.concatenate([first_ref[...], second_ref[...]], axis=0).T
    me = lax.axis_index("seq")
    orders = [y_order(me), y_order(me ^ 1), y_order(me ^ 2), y_order(me ^ 3)[:2], y_order(me ^ 3)[2:]]
    for block, order in zip(blocks, orders):
        place_rows(update_ref, dot_nn(block[...], mix), order)
    embedded = product_tn(embed_ref[...], both_frames(latents_ref))
    gate, shift, scale = modulation_columns(mod_ref[...], (2, 3, 4))
    hidden = embedded + gate * update_ref[...]
    hidden_ref[...] = hidden
    inner_ref[...] = (normalize(hidden) * (1.0 + scale) + shift).astype(BF)


def temporal_kernel(advance_ref, *refs):
    blocks, out_ref = refs[:4], refs[8]
    following = jnp.concatenate([one[...] for one in refs[4:6]], axis=1)
    tokens = jnp.concatenate([one[...] for one in refs[6:8]], axis=1)
    last = lax.axis_index("queue") == lax.axis_size("queue") - 1
    limit = jnp.where(last, 0, advance_ref[0])
    frame = lax.broadcasted_iota(jnp.int32, (1, 128), 1) // 64
    keep_same = frame < limit
    keep_other = (1 - frame) < limit
    scale = math.log2(math.e) / math.sqrt(HD)
    for place, block_ref in enumerate(blocks):
        block = block_ref[0 : 3 * HD]
        both = dot_nn(block, tokens)
        ahead = dot_nn(block[HD : 3 * HD], following)
        query, key, value = (both[HD * index : HD * (index + 1)] for index in range(3))
        key_next, value_next = ahead[0:HD], ahead[HD : 2 * HD]
        for side in range(2):
            lanes = slice(128 * side, 128 * (side + 1))
            asked = query[:, lanes] * scale
            keys = [key[:, lanes], key_next[:, lanes]]
            values = [value[:, lanes], value_next[:, lanes]]
            keys = [keys[0], pltpu.roll(keys[0], 64, 1), keys[1], pltpu.roll(keys[1], 64, 1)]
            values = [values[0], pltpu.roll(values[0], 64, 1), values[1], pltpu.roll(values[1], 64, 1)]
            scores = [jnp.sum(asked * one, axis=0, keepdims=True) for one in keys]
            scores[2] = jnp.where(keep_same, scores[2], -1e30)
            scores[3] = jnp.where(keep_other, scores[3], -1e30)
            top = jnp.maximum(jnp.maximum(scores[0], scores[1]), jnp.maximum(scores[2], scores[3]))
            weights = [jnp.exp2(one - top) for one in scores]
            inverse = 1.0 / (weights[0] + weights[1] + weights[2] + weights[3])
            mixed = sum(w * inverse * v for w, v in zip(weights, values))
            out_ref[HD * place : HD * (place + 1), lanes] = mixed.astype(BF)


def pair_order(me):
    return [index for pair in zip(y_order(me), y_order(me ^ 2)) for index in pair]


def output_kernel(near_ref, across_ref, near_peer_ref, across_peer_ref, *refs):
    blocks, (own_ref, peer_ref, mix_ref) = refs[:4], refs[4:]
    me = lax.axis_index("seq")
    for flip, part in ((0, near_ref), (2, across_ref)):
        place_rows(mix_ref, part[...].astype(F32), y_order(me ^ flip))
    for flip, part in ((1, near_peer_ref), (3, across_peer_ref)):
        value = part[...].astype(F32)
        place_rows(mix_ref, jnp.concatenate([value[:, 128:256], value[:, 0:128]], axis=1), y_order(me ^ flip))
    mix = mix_ref[...].astype(BF)
    for place, block in enumerate(blocks):
        product = dot_nn(block[3 * HD : 5 * HD], mix)
        rows = slice(2 * HD * place, 2 * HD * (place + 1))
        own_ref[rows, :] = product[:, 0:128]
        peer_ref[rows, :] = product[:, 128:256].astype(BF)


def final_kernel(own_ref, peer_ref, hidden_ref, latents_ref, mod_ref, final_ref, velocity_ref, updated_ref, update_ref):
    me = lax.axis_index("seq")
    place_rows(update_ref, own_ref[...], pair_order(me))
    place_rows(update_ref, peer_ref[...].astype(F32), pair_order(me ^ 1))
    gate, shift, scale = modulation_columns(mod_ref[...], (5, 6, 7))
    hidden = hidden_ref[...] + gate * update_ref[...]
    inner = (normalize(hidden) * (1.0 + scale) + shift).astype(BF)
    velocity = dot_nn(final_ref[...], inner)
    for frame in range(2):
        part = velocity[:, 64 * frame : 64 * (frame + 1)]
        velocity_ref[frame] = part
        updated_ref[frame] = latents_ref[frame] - part * (1.0 / 32.0)


def params(mebibytes):
    return pltpu.CompilerParams(vmem_limit_bytes=mebibytes << 20)


def takes(microseconds):
    return pl.CostEstimate(
        flops=int(microseconds * 1.15e9), bytes_accessed=1000, transcendentals=0
    )


def along_seq(array, to):
    return lax.ppermute(array, "seq", [(i, to(i)) for i in range(16)])


def y_up(array):
    return along_seq(array, lambda i: (i + 4) % 16)


def y_down(array):
    return along_seq(array, lambda i: (i + 12) % 16)


def over_x(array):
    return along_seq(array, lambda i: i ^ 2)


def other_core(array):
    return along_seq(array, lambda i: i ^ 1)


def from_next(array):
    return lax.ppermute(array, "queue", [(i, i - 1) for i in range(1, 16)])


def over_both(array):
    return along_seq(array, lambda i: i ^ 3)


def y_far(array):
    return along_seq(array, lambda i: (i + 8) % 16)


def stack_after(after, blocks, name):
    return pl.pallas_call(
        stack_kernel,
        out_shape=jax.ShapeDtypeStruct((len(blocks), *blocks[0].shape), BF),
        in_specs=[VMEM] * (1 + len(blocks)),
        out_specs=VMEM,
        cost_estimate=takes(2),
        name=name,
    )(after, *blocks)


def gate(held, *rows):
    there = rows[0].astype(F32) <= jnp.inf
    for row in rows[1:]:
        there = there & (row.astype(F32) <= jnp.inf)
    return jnp.where(there, held, jnp.zeros_like(held))


def shards(
    latents,
    levels,
    advance,
    fresh_noise,
    level_mod,
    embed_w,
    spatial_qkv,
    spatial_out,
    temporal_qkv,
    temporal_out,
    final_w,
):
    lat = latents.transpose(0, 2, 1)
    spatial_w = spatial_qkv.transpose(1, 0, 2)
    out_w = spatial_out.transpose(1, 0)
    temporal_w = temporal_qkv.transpose(1, 2, 0)
    last_w = temporal_out.transpose(1, 0)
    final_t = final_w.transpose(1, 0)

    with jax.named_scope("last_x"):
        last_across = over_x(last_w)
    packed, scaled = pl.pallas_call(
        pack_kernel,
        out_shape=(
            jax.ShapeDtypeStruct((16, 40, 128), F32),
            jax.ShapeDtypeStruct((16, 128), F32),
        ),
        in_specs=[SMEM, VMEM, VMEM, VMEM, VMEM],
        out_specs=(VMEM, VMEM),
        cost_estimate=takes(2),
        name="pack",
    )(levels, lat, embed_w, level_mod, last_across)
    everyone = lax.all_to_all(packed, "seq", split_axis=0, concat_axis=0, tiled=True)
    with jax.named_scope("out_y"):
        out_far = y_far(out_w)
        out_own = jnp.stack([out_w, y_up(out_w), y_down(out_w), out_far])
    with jax.named_scope("out_x"):
        out_across = over_x(out_own)
    with jax.named_scope("out_core"):
        out_peer = other_core(out_own)
    five = lax.dynamic_update_slice(jnp.zeros((5, HD, D), BF), gate(temporal_w, out_far[0]), (0, 0, 0))
    five = lax.dynamic_update_slice(five, jnp.stack([last_w, last_across]), (3, 0, 0))
    with jax.named_scope("five_y"):
        below, above = y_up(five), y_down(five)

    coef, mod, tokens = pl.pallas_call(
        coefficient_kernel,
        out_shape=(
            jax.ShapeDtypeStruct((2, 3, CP, D), F32),
            jax.ShapeDtypeStruct((16, D), F32),
            jax.ShapeDtypeStruct((2, 16, 1024), F32),
        ),
        in_specs=[VMEM] * 2 + [ANY],
        out_specs=(VMEM, VMEM, VMEM),
        scratch_shapes=[pltpu.VMEM((3, D, D), BF), pltpu.SemaphoreType.DMA((3, 4))],
        compiler_params=params(45),
        cost_estimate=takes(20),
        name="coefficients",
    )(everyone, embed_w, spatial_w)

    def attend(frame, *after):
        return pl.pallas_call(
            functools.partial(attend_kernel, frame),
            out_shape=jax.ShapeDtypeStruct((64, D), BF),
            in_specs=[VMEM] * 3 + [ANY] * len(after),
            out_specs=VMEM,
            scratch_shapes=[
                pltpu.VMEM((CP, 1024), F32),
                pltpu.VMEM((HEADS * CP, 64), F32),
            ],
            compiler_params=params(24),
            cost_estimate=takes(0.1),
            name="attend",
        )(scaled, tokens, coef, *after)

    first = attend(0)
    second = attend(1, first)
    with jax.named_scope("out_core"):
        out_both = [other_core(gate(out_across[half : half + 2], second[0])) for half in (0, 2)]
    first, second = gate(first, below[0, 0]), gate(second, above[0, 0])
    with jax.named_scope("five_far"):
        far = y_far(gate(five, first[0]))

    hidden, inner = pl.pallas_call(
        hidden_kernel,
        out_shape=(
            jax.ShapeDtypeStruct((D, 128), F32),
            jax.ShapeDtypeStruct((D, 128), BF),
        ),
        in_specs=[VMEM] * 10,
        out_specs=(VMEM, VMEM),
        scratch_shapes=[pltpu.VMEM((D, 128), F32)],
        compiler_params=params(24),
        cost_estimate=takes(2),
        name="hidden",
    )(first, second, lat, embed_w, mod, *(one.reshape(-1, D) for one in (out_own, out_peer, out_across, *out_both)))
    with jax.named_scope("inner"):
        pairs = [(16 * q + j, 16 * (q - 1) + (j ^ 2)) for q in range(1, 16) for j in range(16)]
        following_across = lax.ppermute(inner, ("queue", "seq"), pairs)
        across = over_x(inner)
        following = from_next(inner)
    above = gate(above, below[0, 0])
    following_across = gate(following_across, above[0, 0, 0:128])
    with jax.named_scope("inner_core"):
        tokens_four = [inner, other_core(inner), across, other_core(across)]
        following_four = [following, other_core(following), following_across, other_core(following_across)]
    blocks = [one.reshape(5 * HD, D) for one in (five, below, above, far)]

    def temporal(name, *tokens):
        return pl.pallas_call(
            temporal_kernel,
            out_shape=jax.ShapeDtypeStruct((4 * HD, 256), BF),
            in_specs=[SMEM] + [VMEM] * 8,
            out_specs=VMEM,
            compiler_params=params(24),
            cost_estimate=takes(2),
            name=name,
        )(advance, *blocks, *tokens)

    across = temporal("temporal_across", *following_four[2:], *tokens_four[2:])
    near = temporal("temporal_near", *following_four[:2], *tokens_four[:2])
    with jax.named_scope("back"):
        across = over_x(across)
        near_peer, across_peer = other_core(near), other_core(across)
    update_own, update_peer = pl.pallas_call(
        output_kernel,
        out_shape=tuple(jax.ShapeDtypeStruct((8 * HD, 128), kind) for kind in (F32, BF)),
        in_specs=[VMEM] * 8,
        out_specs=(VMEM,) * 2,
        scratch_shapes=[pltpu.VMEM((D, 256), F32)],
        compiler_params=params(24),
        cost_estimate=takes(1),
        name="output",
    )(near, across, near_peer, across_peer, *blocks)
    with jax.named_scope("update"):
        update_peer = other_core(update_peer)
    velocity, updated = pl.pallas_call(
        final_kernel,
        out_shape=(
            jax.ShapeDtypeStruct((2, C, 64), F32),
            jax.ShapeDtypeStruct((2, C, 64), F32),
        ),
        in_specs=[VMEM] * 6,
        out_specs=(VMEM, VMEM),
        scratch_shapes=[pltpu.VMEM((D, 128), F32)],
        compiler_params=params(24),
        cost_estimate=takes(2),
        name="final",
    )(update_own, update_peer, hidden, lat, mod, final_t)
    incoming = from_next(updated[0])
    is_last = lax.axis_index("queue") == lax.axis_size("queue") - 1
    tail = jnp.where(is_last, fresh_noise.transpose(1, 0), incoming)
    queue_next = jnp.stack([updated[1], tail])
    return velocity.transpose(0, 2, 1), queue_next.transpose(0, 2, 1)


def solution(mesh):
    placed = (
        P("queue", "seq", None),
        P("queue"),
        P("queue"),
        P("seq", None),
        P(None, None, "seq"),
        P(),
        P(),
        P(None, "seq"),
        P(None, None, "seq"),
        P(None, "seq"),
        P(),
    )
    return jax.shard_map(
        shards,
        mesh=mesh,
        in_specs=placed,
        out_specs=(P("queue", "seq", None), P("queue", "seq", None)),
        check_vma=False,
    )
```

```python
import functools
import math

import jax
import jax.numpy as jnp
from jax import lax
from jax.experimental import pallas as pl
from jax.experimental.pallas import tpu as pltpu
from jax.sharding import PartitionSpec as P

HEADS = 16
HD = 72
D = HEADS * HD
C = 16
CP = 32
BF = jnp.bfloat16
F32 = jnp.float32
VMEM = pl.BlockSpec(memory_space=pltpu.VMEM)
SMEM = pl.BlockSpec(memory_space=pltpu.SMEM)
ANY = pl.BlockSpec(memory_space=pl.ANY)


def split(value):
    high = value.astype(BF)
    return high, (value - high.astype(F32)).astype(BF)


def dot_tn(a, b):
    return lax.dot_general(a, b, (((0,), (0,)), ((), ())), preferred_element_type=F32)


def dot_nt(a, b):
    return lax.dot_general(a, b, (((1,), (1,)), ((), ())), preferred_element_type=F32)


def dot_nn(a, b):
    return jnp.dot(a, b, preferred_element_type=F32)


def product_tn(a, b):
    a_high, a_low = split(a)
    b_high, b_low = split(b)
    return dot_tn(
        jnp.concatenate([a_high, a_low, a_high], axis=0),
        jnp.concatenate([b_high, b_high, b_low], axis=0),
    )


def both_frames(latents_ref):
    return jnp.concatenate([latents_ref[0], latents_ref[1]], axis=1)


def normalize(hidden):
    width = hidden.shape[0]
    mean_value = jnp.sum(hidden, axis=0, keepdims=True) * (1.0 / width)
    centered = hidden - mean_value
    variance = jnp.sum(centered * centered, axis=0, keepdims=True) * (1.0 / width)
    return centered * lax.rsqrt(variance + 1e-06)


def modulation_columns(mod, rows):
    tokens = 128
    high, low = split(mod)
    row_at = lax.broadcasted_iota(jnp.int32, (16, tokens * len(rows)), 0)
    lane_at = lax.broadcasted_iota(jnp.int32, (16, tokens * len(rows)), 1)
    wanted = jnp.zeros_like(row_at)
    for place, row in enumerate(rows):
        wanted = jnp.where(lane_at // tokens == place, row, wanted)
    wanted = wanted + 8 * ((lane_at % tokens) // 64)
    chosen = (row_at == wanted).astype(F32).astype(BF)
    columns = dot_tn(
        jnp.concatenate([high, low], axis=0), jnp.concatenate([chosen, chosen], axis=0)
    )
    return [columns[:, tokens * i : tokens * (i + 1)] for i in range(len(rows))]


def pack_kernel(levels_ref, latents_ref, embed_ref, table_ref, after_ref, out_ref, own_ref):
    channels = both_frames(latents_ref)
    embed = embed_ref[...]
    centered = embed - jnp.sum(embed, axis=1, keepdims=True) * (1.0 / D)
    spread = product_tn(centered, channels)
    variance = jnp.sum(spread * spread, axis=0, keepdims=True) * (1.0 / D)
    inverse = lax.rsqrt(variance + 1e-06)
    own_ref[...] = channels * inverse
    peers = out_ref.shape[0]
    for peer in range(peers):
        out_ref[peer, 0:16, :] = channels
        out_ref[peer, 32:40, :] = jnp.broadcast_to(inverse, (8, 128))
        for frame in range(2):
            rows = table_ref[levels_ref[frame]]
            out_ref[peer, 16 + 8 * frame : 24 + 8 * frame, 0:HD] = rows


def coefficient_kernel(all_ref, embed_ref, weight_ref, coef_ref, mod_ref, tokens_ref, held_ref, sems):
    parts, rows = sems.shape[1], D // sems.shape[1]
    copies = [
        [
            pltpu.make_async_copy(
                weight_ref.at[index, pl.ds(rows * part, rows)],
                held_ref.at[index, pl.ds(rows * part, rows)],
                sems.at[index, part],
            )
            for part in range(parts)
        ]
        for index in range(3)
    ]
    for index in range(3):
        for copy in copies[index]:
            copy.start()
    peers = all_ref.shape[0]
    for peer in range(peers):
        mod_ref[:, HD * peer : HD * (peer + 1)] = all_ref[peer, 16:32, 0:HD]
        scaled = all_ref[peer, 0:16] * all_ref[peer, 32:33]
        for frame in range(2):
            tokens_ref[frame, :, 64 * peer : 64 * (peer + 1)] = scaled[:, 64 * frame : 64 * (frame + 1)]
    mod = mod_ref[...]
    embed = embed_ref[...]
    centered = embed - jnp.sum(embed, axis=1, keepdims=True) * (1.0 / D)
    row16 = lax.broadcasted_iota(jnp.int32, (16, D), 0)
    rows = []
    for frame in range(2):
        rows.append(centered * (1.0 + mod[8 * frame + 1 : 8 * frame + 2]))
        rows.append(jnp.where(row16 == 0, mod[8 * frame : 8 * frame + 1], 0.0))
    high, low = split(jnp.concatenate(rows, axis=0))
    stacked = jnp.concatenate([high, low], axis=0)
    for index in range(3):
        for copy in copies[index]:
            copy.wait()
        both = dot_nn(stacked, held_ref[index])
        for frame in range(2):
            rows = slice(CP * frame, CP * (frame + 1))
            coef_ref[frame, index] = both[rows] + both[64:128][rows]


def attend_kernel(frame, own_ref, tokens_ref, coef_ref, *refs):
    mix_ref, query_ref, part_ref = refs[-3:]
    own_head = (
        lax.broadcasted_iota(jnp.int32, (HEADS * CP, D), 0) // CP
        == lax.broadcasted_iota(jnp.int32, (HEADS * CP, D), 1) // HD
    )
    scale = math.log2(math.e) / math.sqrt(HD)
    one_row = (lax.broadcasted_iota(jnp.int32, (16, 64), 0) == 0).astype(F32)
    one_row_all = (lax.broadcasted_iota(jnp.int32, (16, 1024), 0) == 0).astype(F32)
    key_heads = jnp.where(own_head, jnp.concatenate([coef_ref[frame, 1]] * HEADS, axis=0), 0.0).astype(BF)
    pair = dot_nt(key_heads, coef_ref[frame, 0].astype(BF)) * scale
    own = jnp.concatenate([own_ref[:, 64 * frame : 64 * (frame + 1)], one_row], axis=0)
    own_high, own_low = split(own)
    pair_high, pair_low = split(pair)
    reduced = dot_nn(
        jnp.concatenate([pair_high, pair_low, pair_high], axis=1),
        jnp.concatenate([own_high, own_high, own_low], axis=0),
    )
    for head in range(HEADS):
        query_ref[:, 64 * head : 64 * (head + 1)] = reduced[CP * head : CP * (head + 1)]
    query_high, query_low = split(query_ref[...])
    queries = jnp.concatenate([query_high, query_low, query_high], axis=0)
    token_high, token_low = split(jnp.concatenate([tokens_ref[frame], one_row_all], axis=0))
    keys = jnp.concatenate([token_high, token_high, token_low], axis=0)
    values = jnp.concatenate([token_high, token_low[0:16]], axis=0)
    for chunk in range(2):
        scores = dot_tn(keys, queries[:, 512 * chunk : 512 * (chunk + 1)])
        top = jnp.max(scores, axis=0, keepdims=True)
        weights = jnp.exp2(scores - top).astype(BF)
        summed = dot_nn(values, weights)
        mixed = (summed[0:16] + summed[32:48]) / summed[16:17]
        for sub in range(8):
            head = 8 * chunk + sub
            part_ref[CP * head : CP * head + 16, :] = mixed[:, 64 * sub : 64 * (sub + 1)]
            part_ref[CP * head + 16 : CP * head + 32, :] = one_row
    value_heads = jnp.where(own_head, jnp.concatenate([coef_ref[frame, 2]] * HEADS, axis=0), 0.0).astype(BF)
    mix_ref[...] = dot_tn(part_ref[...].astype(BF), value_heads).astype(BF)


def y_order(me):
    return [me, lax.rem(me + 12, 16), lax.rem(me + 4, 16), lax.rem(me + 8, 16)]


def at_rows(index):
    return pl.ds(pl.multiple_of(index * HD, 8), HD)


def place_rows(out_ref, product, order):
    for place, index in enumerate(order):
        out_ref[at_rows(index), :] = product[HD * place : HD * (place + 1)]


def hidden_kernel(first_ref, second_ref, latents_ref, embed_ref, mod_ref, *rest):
    *blocks, hidden_ref, inner_ref, update_ref = rest
    mix = jnp.concatenate([first_ref[...], second_ref[...]], axis=0).T
    me = lax.axis_index("seq")
    orders = [y_order(me), y_order(me ^ 1), y_order(me ^ 2), y_order(me ^ 3)[:2], y_order(me ^ 3)[2:]]
    for block, order in zip(blocks, orders):
        place_rows(update_ref, dot_nn(block[...], mix), order)
    embedded = product_tn(embed_ref[...], both_frames(latents_ref))
    gate, shift, scale = modulation_columns(mod_ref[...], (2, 3, 4))
    hidden = embedded + gate * update_ref[...]
    hidden_ref[...] = hidden
    inner_ref[...] = (normalize(hidden) * (1.0 + scale) + shift).astype(BF)


def temporal_kernel(advance_ref, *refs):
    blocks, out_ref = refs[:4], refs[8]
    following = jnp.concatenate([one[...] for one in refs[4:6]], axis=1)
    tokens = jnp.concatenate([one[...] for one in refs[6:8]], axis=1)
    last = lax.axis_index("queue") == lax.axis_size("queue") - 1
    limit = jnp.where(last, 0, advance_ref[0])
    frame = lax.broadcasted_iota(jnp.int32, (1, 128), 1) // 64
    keep_same = frame < limit
    keep_other = (1 - frame) < limit
    scale = math.log2(math.e) / math.sqrt(HD)
    for place, block_ref in enumerate(blocks):
        block = block_ref[0 : 3 * HD]
        both = dot_nn(block, tokens)
        ahead = dot_nn(block[HD : 3 * HD], following)
        query, key, value = (both[HD * index : HD * (index + 1)] for index in range(3))
        key_next, value_next = ahead[0:HD], ahead[HD : 2 * HD]
        for side in range(2):
            lanes = slice(128 * side, 128 * (side + 1))
            asked = query[:, lanes] * scale
            keys = [key[:, lanes], key_next[:, lanes]]
            values = [value[:, lanes], value_next[:, lanes]]
            keys = [keys[0], pltpu.roll(keys[0], 64, 1), keys[1], pltpu.roll(keys[1], 64, 1)]
            values = [values[0], pltpu.roll(values[0], 64, 1), values[1], pltpu.roll(values[1], 64, 1)]
            scores = [jnp.sum(asked * one, axis=0, keepdims=True) for one in keys]
            scores[2] = jnp.where(keep_same, scores[2], -1e30)
            scores[3] = jnp.where(keep_other, scores[3], -1e30)
            top = jnp.maximum(jnp.maximum(scores[0], scores[1]), jnp.maximum(scores[2], scores[3]))
            weights = [jnp.exp2(one - top) for one in scores]
            inverse = 1.0 / (weights[0] + weights[1] + weights[2] + weights[3])
            mixed = sum(w * inverse * v for w, v in zip(weights, values))
            out_ref[HD * place : HD * (place + 1), lanes] = mixed.astype(BF)


def pair_order(me):
    return [index for pair in zip(y_order(me), y_order(me ^ 2)) for index in pair]


def output_kernel(near_ref, across_ref, near_peer_ref, across_peer_ref, *refs):
    blocks, (own_ref, peer_ref, mix_ref) = refs[:4], refs[4:]
    me = lax.axis_index("seq")
    for flip, part in ((0, near_ref), (2, across_ref)):
        place_rows(mix_ref, part[...].astype(F32), y_order(me ^ flip))
    for flip, part in ((1, near_peer_ref), (3, across_peer_ref)):
        value = part[...].astype(F32)
        place_rows(mix_ref, jnp.concatenate([value[:, 128:256], value[:, 0:128]], axis=1), y_order(me ^ flip))
    mix = mix_ref[...].astype(BF)
    for place, block in enumerate(blocks):
        product = dot_nn(block[3 * HD : 5 * HD], mix)
        rows = slice(2 * HD * place, 2 * HD * (place + 1))
        own_ref[rows, :] = product[:, 0:128]
        peer_ref[rows, :] = product[:, 128:256].astype(BF)


def final_kernel(own_ref, peer_ref, hidden_ref, latents_ref, mod_ref, final_ref, velocity_ref, updated_ref, update_ref):
    me = lax.axis_index("seq")
    place_rows(update_ref, own_ref[...], pair_order(me))
    place_rows(update_ref, peer_ref[...].astype(F32), pair_order(me ^ 1))
    gate, shift, scale = modulation_columns(mod_ref[...], (5, 6, 7))
    hidden = hidden_ref[...] + gate * update_ref[...]
    inner = (normalize(hidden) * (1.0 + scale) + shift).astype(BF)
    velocity = dot_nn(final_ref[...], inner)
    for frame in range(2):
        part = velocity[:, 64 * frame : 64 * (frame + 1)]
        velocity_ref[frame] = part
        updated_ref[frame] = latents_ref[frame] - part * (1.0 / 32.0)


def params(mebibytes):
    return pltpu.CompilerParams(vmem_limit_bytes=mebibytes << 20)


def takes(microseconds):
    return pl.CostEstimate(
        flops=int(microseconds * 1.15e9), bytes_accessed=1000, transcendentals=0
    )


def along_seq(array, to):
    return lax.ppermute(array, "seq", [(i, to(i)) for i in range(16)])


def y_up(array):
    return along_seq(array, lambda i: (i + 4) % 16)


def y_down(array):
    return along_seq(array, lambda i: (i + 12) % 16)


def over_x(array):
    return along_seq(array, lambda i: i ^ 2)


def other_core(array):
    return along_seq(array, lambda i: i ^ 1)


def from_next(array):
    return lax.ppermute(array, "queue", [(i, i - 1) for i in range(1, 16)])


def over_both(array):
    return along_seq(array, lambda i: i ^ 3)


def y_far(array):
    return along_seq(array, lambda i: (i + 8) % 16)


def stack_after(after, blocks, name):
    return pl.pallas_call(
        stack_kernel,
        out_shape=jax.ShapeDtypeStruct((len(blocks), *blocks[0].shape), BF),
        in_specs=[VMEM] * (1 + len(blocks)),
        out_specs=VMEM,
        cost_estimate=takes(2),
        name=name,
    )(after, *blocks)


def gate(held, *rows):
    there = rows[0].astype(F32) <= jnp.inf
    for row in rows[1:]:
        there = there & (row.astype(F32) <= jnp.inf)
    return jnp.where(there, held, jnp.zeros_like(held))


def shards(
    latents,
    levels,
    advance,
    fresh_noise,
    level_mod,
    embed_w,
    spatial_qkv,
    spatial_out,
    temporal_qkv,
    temporal_out,
    final_w,
):
    lat = latents.transpose(0, 2, 1)
    spatial_w = spatial_qkv.transpose(1, 0, 2)
    out_w = spatial_out.transpose(1, 0)
    temporal_w = temporal_qkv.transpose(1, 2, 0)
    last_w = temporal_out.transpose(1, 0)
    final_t = final_w.transpose(1, 0)

    with jax.named_scope("last_x"):
        last_across = over_x(last_w)
    packed, scaled = pl.pallas_call(
        pack_kernel,
        out_shape=(
            jax.ShapeDtypeStruct((16, 40, 128), F32),
            jax.ShapeDtypeStruct((16, 128), F32),
        ),
        in_specs=[SMEM, VMEM, VMEM, VMEM, VMEM],
        out_specs=(VMEM, VMEM),
        cost_estimate=takes(2),
        name="pack",
    )(levels, lat, embed_w, level_mod, last_across)
    everyone = lax.all_to_all(packed, "seq", split_axis=0, concat_axis=0, tiled=True)
    with jax.named_scope("out_y"):
        out_far = y_far(out_w)
        out_own = jnp.stack([out_w, y_up(out_w), y_down(out_w), out_far])
    with jax.named_scope("out_x"):
        out_across = over_x(out_own)
    with jax.named_scope("out_core"):
        out_peer = other_core(out_own)
    five = lax.dynamic_update_slice(jnp.zeros((5, HD, D), BF), gate(temporal_w, out_far[0]), (0, 0, 0))
    five = lax.dynamic_update_slice(five, jnp.stack([last_w, last_across]), (3, 0, 0))
    with jax.named_scope("five_y"):
        below, above = y_up(five), y_down(five)

    coef, mod, tokens = pl.pallas_call(
        coefficient_kernel,
        out_shape=(
            jax.ShapeDtypeStruct((2, 3, CP, D), F32),
            jax.ShapeDtypeStruct((16, D), F32),
            jax.ShapeDtypeStruct((2, 16, 1024), F32),
        ),
        in_specs=[VMEM] * 2 + [ANY],
        out_specs=(VMEM, VMEM, VMEM),
        scratch_shapes=[pltpu.VMEM((3, D, D), BF), pltpu.SemaphoreType.DMA((3, 4))],
        compiler_params=params(45),
        cost_estimate=takes(20),
        name="coefficients",
    )(everyone, embed_w, spatial_w)

    def attend(frame, *after):
        return pl.pallas_call(
            functools.partial(attend_kernel, frame),
            out_shape=jax.ShapeDtypeStruct((64, D), BF),
            in_specs=[VMEM] * 3 + [ANY] * len(after),
            out_specs=VMEM,
            scratch_shapes=[
                pltpu.VMEM((CP, 1024), F32),
                pltpu.VMEM((HEADS * CP, 64), F32),
            ],
            compiler_params=params(24),
            cost_estimate=takes(0.1),
            name="attend",
        )(scaled, tokens, coef, *after)

    first = attend(0)
    second = attend(1, first)
    with jax.named_scope("out_core"):
        out_both = [other_core(gate(out_across[half : half + 2], second[0])) for half in (0, 2)]
    first, second = gate(first, below[0, 0]), gate(second, above[0, 0])
    with jax.named_scope("five_far"):
        far = y_far(gate(five, first[0]))

    hidden, inner = pl.pallas_call(
        hidden_kernel,
        out_shape=(
            jax.ShapeDtypeStruct((D, 128), F32),
            jax.ShapeDtypeStruct((D, 128), BF),
        ),
        in_specs=[VMEM] * 10,
        out_specs=(VMEM, VMEM),
        scratch_shapes=[pltpu.VMEM((D, 128), F32)],
        compiler_params=params(24),
        cost_estimate=takes(2),
        name="hidden",
    )(first, second, lat, embed_w, mod, *(one.reshape(-1, D) for one in (out_own, out_peer, out_across, *out_both)))
    with jax.named_scope("inner"):
        pairs = [(16 * q + j, 16 * (q - 1) + (j ^ 2)) for q in range(1, 16) for j in range(16)]
        following_across = lax.ppermute(inner, ("queue", "seq"), pairs)
        across = over_x(inner)
        following = from_next(inner)
    above = gate(above, below[0, 0])
    following_across = gate(following_across, above[0, 0, 0:128])
    with jax.named_scope("inner_core"):
        tokens_four = [inner, other_core(inner), across, other_core(across)]
        following_four = [following, other_core(following), following_across, other_core(following_across)]
    blocks = [one.reshape(5 * HD, D) for one in (five, below, above, far)]

    def temporal(name, *tokens):
        return pl.pallas_call(
            temporal_kernel,
            out_shape=jax.ShapeDtypeStruct((4 * HD, 256), BF),
            in_specs=[SMEM] + [VMEM] * 8,
            out_specs=VMEM,
            compiler_params=params(24),
            cost_estimate=takes(2),
            name=name,
        )(advance, *blocks, *tokens)

    across = temporal("temporal_across", *following_four[2:], *tokens_four[2:])
    near = temporal("temporal_near", *following_four[:2], *tokens_four[:2])
    with jax.named_scope("back"):
        across = over_x(across)
        near_peer, across_peer = other_core(near), other_core(across)
    update_own, update_peer = pl.pallas_call(
        output_kernel,
        out_shape=tuple(jax.ShapeDtypeStruct((8 * HD, 128), kind) for kind in (F32, BF)),
        in_specs=[VMEM] * 8,
        out_specs=(VMEM,) * 2,
        scratch_shapes=[pltpu.VMEM((D, 256), F32)],
        compiler_params=params(24),
        cost_estimate=takes(1),
        name="output",
    )(near, across, near_peer, across_peer, *blocks)
    with jax.named_scope("update"):
        update_peer = other_core(update_peer)
    velocity, updated = pl.pallas_call(
        final_kernel,
        out_shape=(
            jax.ShapeDtypeStruct((2, C, 64), F32),
            jax.ShapeDtypeStruct((2, C, 64), F32),
        ),
        in_specs=[VMEM] * 6,
        out_specs=(VMEM, VMEM),
        scratch_shapes=[pltpu.VMEM((D, 128), F32)],
        compiler_params=params(24),
        cost_estimate=takes(2),
        name="final",
    )(update_own, update_peer, hidden, lat, mod, final_t)
    incoming = from_next(updated[0])
    is_last = lax.axis_index("queue") == lax.axis_size("queue") - 1
    tail = jnp.where(is_last, fresh_noise.transpose(1, 0), incoming)
    queue_next = jnp.stack([updated[1], tail])
    return velocity.transpose(0, 2, 1), queue_next.transpose(0, 2, 1)


def solution(mesh):
    placed = (
        P("queue", "seq", None),
        P("queue"),
        P("queue"),
        P("seq", None),
        P(None, None, "seq"),
        P(),
        P(),
        P(None, "seq"),
        P(None, None, "seq"),
        P(None, "seq"),
        P(),
    )
    return jax.shard_map(
        shards,
        mesh=mesh,
        in_specs=placed,
        out_specs=(P("queue", "seq", None), P("queue", "seq", None)),
        check_vma=False,
    )
```
